256 devices in a mesh: src: 64 (over x, z, y_lo), rcv: 4 (over y_hi, core).
Axes of the slice: x: 4, y: 4 (y_hi: 2, y_lo: 2; y = y_hi * 2 + y_lo), z: 8, core: 2. Of those that a mesh axis runs over, the one named last changes fastest.
Arguments:
- spectra: float32 [2, 4, 4096, 4096], P(None, None, 'src', 'rcv'), may hold values from -6 to 6
- panels: int32 [2], replicated, may hold values from 0 to 63, as said below
- filters: float32 [4096, 64], P('src'), may hold values from -0.036 to 0.036
- offsets: int32 [4096], P('src'), may hold values from 63 to 2040
Outputs:
- primaries: bfloat16 [8, 4096, 4096], P(None, 'src', 'rcv')
The draws below stay inside these ranges and needn't reach their ends.
Inputs may be any that keep to these rules, and one draw needn't show every extreme that they name: `panels`: 2 different panel numbers, one of them 64 - 1.
All inputs are finite; a program needn't handle non-finite values.
Results may differ from the reference program's by a relative error of at most 0.001.
Values sent between devices are 32-bit elements; how exact they have to be, the bound alone decides.
No kernel may reach another device: no remote copies, remote signals or barrier semaphores. Data moves between devices by JAX's collectives and lax.ppermute only.
A program may use at most 64 MiB of HBM per device.

```python
import math
import jax
import jax.numpy as jnp
from jax import lax

SHOT_DEV = 64
FREQ = 4
TWIN = 8
TAPS = 64
NPAN = 2
NT = 2048
FIRST_BIN = 64
SHOTS = 4096
NPANELS = 64


def draw_panels(key, part):
    others = jax.random.permutation(jax.random.fold_in(key, 11), NPANELS - 1)[:NPAN - 1].astype(jnp.int32)
    listed = jnp.concatenate([others, jnp.full((1,), NPANELS - 1, jnp.int32)])
    place = jax.random.randint(jax.random.fold_in(key, 12), (), 0, NPAN)
    return jnp.roll(listed, place).astype(jnp.int32)


def place_ends(entries, stream_key, least, top_value):
    spot = [jax.random.randint(jax.random.fold_in(stream_key, axis), (), 0, length) for axis, length in enumerate(entries.shape)]
    widest = entries.shape.index(max(entries.shape))
    next_to = spot[:widest] + [(spot[widest] + 1) % entries.shape[widest]] + spot[widest + 1:]
    return entries.at[tuple(spot)].set(least).at[tuple(next_to)].set(top_value)


def block_levels(stream_key, shape, split, least, high):
    gain = 1.0
    for dim, blocks in split:
        steps = jax.random.uniform(jax.random.fold_in(jax.random.fold_in(stream_key, 6), dim), (blocks,), jnp.float32, least / len(split), high / len(split))
        gain = gain * jnp.repeat(jnp.exp(steps), shape[dim] // blocks).reshape((-1,) + (1,) * (len(shape) - 1 - dim))
    return gain


def scatter_about(rng, shape, spread, bound, shards=(), kind=jnp.bfloat16):
    level = block_levels(rng, shape, shards, -0.22, 0.18) if shards else 1.0
    values = jax.random.normal(rng, shape, jnp.float32) * spread * level
    return jnp.minimum(jnp.maximum(values, -bound), bound).astype(kind)


def setup_inputs(seed: int = 0) -> dict:
    key_list = jax.random.split(jax.random.key(seed), 5)
    return {
        "spectra": scatter_about(key_list[0], (2, FREQ, SHOTS, SHOTS), 1.0, 6.0, ((2, 64), (3, 4)), jnp.float32),
        "panels": draw_panels(jax.random.fold_in(key_list[4], 71), 0),
        "filters": scatter_about(key_list[2], (SHOTS, TAPS), 0.006, 0.036, ((0, 64),), jnp.float32),
        "offsets": place_ends(jax.random.randint(key_list[3], (SHOTS,), TAPS - 1, NT - TWIN + 1), jax.random.fold_in(key_list[3], 1), TAPS - 1, NT - TWIN).astype(jnp.int32),
    }


def complex_product(column_band, row_group_block):
    upper_limit = lax.Precision.HIGHEST
    real_component = jnp.einsum("xcy,xye->xce", column_band[0], row_group_block[0], precision=upper_limit) - jnp.einsum("xcy,xye->xce", column_band[1], row_group_block[1], precision=upper_limit)
    imaginary_component = jnp.einsum("xcy,xye->xce", column_band[0], row_group_block[1], precision=upper_limit) + jnp.einsum("xcy,xye->xce", column_band[1], row_group_block[0], precision=upper_limit)
    return jnp.stack([real_component, imaginary_component])


def phase_tables(offsets, sample_count, shift, freq_count):
    sample_times = offsets[:, None] + shift + jnp.arange(sample_count, dtype=jnp.int32)[None, :]
    bin_numbers = FIRST_BIN + jnp.arange(freq_count, dtype=jnp.int32)
    phase_index = (sample_times[:, :, None] * bin_numbers[None, None, :]) % NT
    angles = phase_index.astype(jnp.float32) * (2.0 * math.pi / NT)
    return jnp.cos(angles), jnp.sin(angles)


def tap_matrix(filters, out_count):
    taps = filters.shape[1]
    out_time = jnp.arange(out_count, dtype=jnp.int32)[:, None]
    sample_lag = jnp.arange(out_count + taps - 1, dtype=jnp.int32)[None, :]
    tap_index = out_time + taps - 1 - sample_lag
    one_hot = (tap_index[:, :, None] == jnp.arange(taps, dtype=jnp.int32)[None, None, :]).astype(jnp.float32)
    return jnp.einsum("sj,tlj->stl", filters, one_hot, precision=lax.Precision.HIGHEST)


def time_rows(frequency_spectrum, gather_record, filters, offsets):
    upper_limit = lax.Precision.HIGHEST
    freq_count = frequency_spectrum.shape[1]
    taps = filters.shape[1]
    cosine_predicted, sine_predicted = phase_tables(offsets, TWIN + taps - 1, 1 - taps, freq_count)
    cosine_recorded, sine_recorded = phase_tables(offsets, TWIN, 0, freq_count)
    recorded_data = jnp.einsum("phk,hmp->mhk", gather_record[0], cosine_recorded, precision=upper_limit) - jnp.einsum("phk,hmp->mhk", gather_record[1], sine_recorded, precision=upper_limit)
    tap_table = tap_matrix(filters, TWIN)
    predicted_multiples = jnp.einsum("tvu,vnt->vnu", frequency_spectrum[0], cosine_predicted, precision=upper_limit) - jnp.einsum("tvu,vnt->vnu", frequency_spectrum[1], sine_predicted, precision=upper_limit)
    filtered = jnp.einsum("stl,slr->tsr", tap_table, predicted_multiples, precision=upper_limit)
    return recorded_data - filtered


def time_output(frequency_spectrum, gather_record, filters, offsets):
    row_count = frequency_spectrum.shape[2]
    block_rows = math.gcd(16, row_count)

    def one_block(block_index):
        first_row = block_index * block_rows
        spec_rows = lax.dynamic_slice_in_dim(frequency_spectrum, first_row, block_rows, 2)
        rec_rows = lax.dynamic_slice_in_dim(gather_record, first_row, block_rows, 2)
        filt_rows = lax.dynamic_slice_in_dim(filters, first_row, block_rows, 0)
        off_rows = lax.dynamic_slice_in_dim(offsets, first_row, block_rows, 0)
        return time_rows(spec_rows, rec_rows, filt_rows, off_rows)

    stacked = lax.map(one_block, jnp.arange(row_count // block_rows, dtype=jnp.int32))
    return jnp.transpose(stacked, (1, 0, 2, 3)).reshape(TWIN, row_count, frequency_spectrum.shape[3])


def reference(spectra, panels, filters, offsets):
    def shot_block(block_index):
        first_row = block_index * SHOT_DEV
        own_rows = lax.dynamic_slice_in_dim(spectra, first_row, SHOT_DEV, 2)
        frequency_spectrum = jnp.zeros((2, FREQ, SHOT_DEV, SHOTS), jnp.float32)
        for panel_step in range(NPAN):
            panel_start = (panels[panel_step] * SHOT_DEV).astype(jnp.int32)
            column_band = lax.dynamic_slice_in_dim(own_rows, panel_start, SHOT_DEV, 3)
            row_group_block = lax.dynamic_slice_in_dim(spectra, panel_start, SHOT_DEV, 2)
            frequency_spectrum = frequency_spectrum + complex_product(column_band, row_group_block)
        filt_rows = lax.dynamic_slice_in_dim(filters, first_row, SHOT_DEV, 0)
        off_rows = lax.dynamic_slice_in_dim(offsets, first_row, SHOT_DEV, 0)
        return time_output(frequency_spectrum, own_rows, filt_rows, off_rows).astype(jnp.bfloat16)

    stacked = lax.map(shot_block, jnp.arange(SHOTS // SHOT_DEV, dtype=jnp.int32))
    return jnp.transpose(stacked, (1, 0, 2, 3)).reshape(TWIN, SHOTS, SHOTS)
```

```python
import math

import jax
import jax.numpy as jnp
import numpy as np
from jax import lax
from jax.experimental import pallas as pl
from jax.experimental.pallas import tpu as pltpu
from jax.sharding import Mesh
from jax.sharding import PartitionSpec as P

TWIN = 8
NT = 2048
FIRST_BIN = 64
FREQ = 4
ROWS = 64
COLS = 1024
LAST = 63
HI = lax.Precision.HIGHEST


def place_of(panel):
    return panel // 16, (panel // 2) % 8, panel % 2


def line_broadcast(v, root, z):
    def at(k):
        return (root + k) % 8

    held = jnp.where(z == root, v, jnp.zeros_like(v))
    up = lax.ppermute(v, "z", [(root, at(3))])
    down = lax.ppermute(v, "z", [(root, at(-3))])
    held = held + up + down
    near = lax.ppermute(held, "z", [(root, at(1)), (at(3), at(2)), (at(-3), at(-2))])
    far = lax.ppermute(held, "z", [(root, at(-1)), (at(3), at(4))])
    return held + near + far


def strips(spectra, panels):
    flat = spectra.reshape(2 * FREQ, ROWS, COLS)
    lane_panel = lax.broadcasted_iota(jnp.int32, (1, 1, 2 * ROWS), 2) // ROWS
    picked = [
        lax.dynamic_slice_in_dim(flat, (panels[i] % 16) * ROWS, ROWS, 2) for i in range(2)
    ]
    block = jnp.concatenate(picked, axis=2)
    owners = panels // 16
    for axis, bit in (("c", owners % 2), ("yh", owners // 2)):
        other = lax.ppermute(block, axis, [(0, 1), (1, 0)])
        keep = jnp.where(lane_panel == 0, bit[0], bit[1]) == lax.axis_index(axis)
        block = jnp.where(keep, block, other)
    return block.reshape(2, FREQ, ROWS, 2 * ROWS)


def kernel(bins, x_ref, l_ref, coef_ref, *refs):
    block_refs, o_ref = refs[:-1], refs[-1]
    total = [None] * TWIN
    for i in range(4):
        own, partner = block_refs[2 * i], block_refs[2 * i + 1]
        cols = own.shape[-1]
        b = jnp.concatenate(
            [own[...].reshape(2 * ROWS, cols), partner[...].reshape(2 * ROWS, cols)], axis=0
        )
        high = b.astype(jnp.bfloat16)
        low = (b - high.astype(jnp.float32)).astype(jnp.bfloat16)
        left = l_ref[bins[i]]
        left_high = left.astype(jnp.bfloat16)
        left_low = (left - left_high.astype(jnp.float32)).astype(jnp.bfloat16)
        product = (
            jnp.dot(left_low, high, preferred_element_type=jnp.float32)
            + jnp.dot(left_high, low, preferred_element_type=jnp.float32)
            + jnp.dot(left_high, high, preferred_element_type=jnp.float32)
        )
        f = bins[i]
        real = x_ref[0, f] - product[:ROWS]
        imag = x_ref[1, f] - product[ROWS:]
        for u in range(TWIN):
            at = u * 8 + i * 2
            term = real * coef_ref[:, at : at + 1] - imag * coef_ref[:, at + 1 : at + 2]
            total[u] = term if total[u] is None else total[u] + term
    for u in range(TWIN):
        o_ref[u] = total[u].astype(o_ref.dtype)


def synthesise(bins, spectra, left, coefs, blocks):
    width = 256
    block_spec = pl.BlockSpec((2, ROWS, width), lambda j, bins: (0, 0, j))
    grid_spec = pltpu.PrefetchScalarGridSpec(
        num_scalar_prefetch=1,
        grid=(COLS // width,),
        in_specs=[
            pl.BlockSpec((2, FREQ, ROWS, width), lambda j, bins: (0, 0, 0, j)),
            pl.BlockSpec((4, 128, 256), lambda j, bins: (0, 0, 0)),
            pl.BlockSpec((ROWS, 64), lambda j, bins: (0, 0)),
            *[block_spec] * 8,
        ],
        out_specs=pl.BlockSpec((TWIN, ROWS, width), lambda j, bins: (0, 0, j)),
    )
    return pl.pallas_call(
        kernel,
        grid_spec=grid_spec,
        out_shape=jax.ShapeDtypeStruct((TWIN, ROWS, COLS), jnp.bfloat16),
        compiler_params=pltpu.CompilerParams(vmem_limit_bytes=40 * 1024 * 1024),
        cost_estimate=pl.CostEstimate(
            flops=2 * 3 * 4 * 128 * 256 * COLS, bytes_accessed=8 * 2**20, transcendentals=0
        ),
    )(bins, spectra, left, coefs, *blocks)


def tables(filters, offsets, strip, bins, yl):
    lag = np.arange(64, dtype=np.int64)[:, None] * (FIRST_BIN + np.arange(FREQ))[None, :] % NT
    lag_angle = lag * (2.0 * math.pi / NT)
    response_cos = jnp.dot(filters, jnp.asarray(np.cos(lag_angle), jnp.float32), precision=HI)
    response_sin = jnp.dot(filters, jnp.asarray(np.sin(lag_angle), jnp.float32), precision=HI)
    a_real, a_imag = strip[0], strip[1]
    rc, rs = response_cos.T[:, :, None], response_sin.T[:, :, None]
    real = a_real * rc + a_imag * rs
    imag = a_imag * rc - a_real * rs
    re_first = jnp.concatenate([real, -imag], axis=2)
    im_first = jnp.concatenate([imag, real], axis=2)
    re_last = jnp.concatenate([-imag, real], axis=2)
    im_last = jnp.concatenate([real, imag], axis=2)
    left = jnp.where(
        yl == 0,
        jnp.concatenate([re_first, im_first], axis=1),
        jnp.concatenate([re_last, im_last], axis=1),
    )
    times = offsets[:, None] + jnp.arange(TWIN, dtype=jnp.int32)[None, :]
    phase = times[:, :, None] * (FIRST_BIN + bins)[None, None, :] % NT
    angle = phase.astype(jnp.float32) * (2.0 * math.pi / NT)
    coefs = jnp.stack([jnp.cos(angle), jnp.sin(angle)], axis=3).reshape(ROWS, 64)
    return left, coefs


def shards(spectra, panels, filters, offsets):
    x, z, yl = lax.axis_index("x"), lax.axis_index("z"), lax.axis_index("yl")
    strip = strips(spectra, panels)
    slot = jnp.where(panels[0] == LAST, 0, 1)
    other = jnp.where(panels[0] == LAST, panels[1], panels[0])
    members = [(f - 2 * c) % 4 * 2 + c for c in range(2) for f in range(4)]
    flat = spectra.reshape(2 * FREQ, ROWS, COLS)
    arrived = lax.all_to_all(
        flat, ("x", "yl"), 0, 0, axis_index_groups=[members], tiled=True
    )
    ox, oz, oy = place_of(other)
    lx, lz, ly = place_of(LAST)
    mine = lax.dynamic_index_in_dim(arrived, oy * 4 + (ox + 2 * oy) % 4, 0, keepdims=False)
    last = arrived[ly * 4 + (lx + 2 * ly) % 4]

    def branch(root):
        return lambda a, b: (line_broadcast(a, root, z), line_broadcast(b, lz, z))

    mine, last = lax.switch(oz, [branch(r) for r in range(8)], mine, last)
    own = jnp.where(slot == 0, jnp.stack([last, mine]), jnp.stack([mine, last]))
    plane = [(i, j) for i in range(4) for j in range(2)]
    across = [(i * 2 + j, ((i + 2) % 4) * 2 + 1 - j) for i, j in plane]
    partner = lax.ppermute(own, ("x", "yl"), across)
    blocks = [own, partner]
    turn = [(i, (i + 1) % 4) for i in range(4)]
    back = [(i, (i - 1) % 4) for i in range(4)]
    for axis, pairs in (("yl", [(0, 1), (1, 0)]), ("x", turn), ("x", back)):
        for v in (own, partner):
            blocks.append(lax.ppermute(v, axis, pairs))
    blocks[2], blocks[3] = blocks[3], blocks[2]
    mine_bin = (x + 2 * yl) % 4
    bins = (mine_bin + jnp.array([0, 2, 3, 1], jnp.int32)) % 4
    left, coefs = tables(filters, offsets, strip, bins, yl)
    return synthesise(bins, spectra, left, coefs, blocks)


def solution(mesh):
    fine = Mesh(mesh.devices.reshape(4, 8, 2, 2, 2), ("x", "z", "yl", "yh", "c"))
    src, rcv = ("x", "z", "yl"), ("yh", "c")
    return jax.shard_map(
        shards,
        mesh=fine,
        in_specs=(P(None, None, src, rcv), P(), P(src, None), P(src)),
        out_specs=P(None, src, rcv),
        check_vma=False,
    )
```

```python
import math

import jax
import jax.numpy as jnp
import numpy as np
from jax import lax
from jax.experimental import pallas as pl
from jax.experimental.pallas import tpu as pltpu
from jax.sharding import Mesh
from jax.sharding import PartitionSpec as P

TWIN = 8
NT = 2048
FIRST_BIN = 64
FREQ = 4
ROWS = 64
COLS = 1024
LAST = 63
HI = lax.Precision.HIGHEST


def place_of(panel):
    return panel // 16, (panel // 2) % 8, panel % 2


def leap(v, group):
    roots = (group, group + 4)
    up = lax.ppermute(v, "z", [(r, (r + 3) % 8) for r in roots])
    down = lax.ppermute(v, "z", [(r, (r - 3) % 8) for r in roots])
    return up, down


def line_broadcast(blocks, roots, z):
    def branch(group):
        return lambda a, b: (leap(a, group), leap(b, LAST // 2 % 4))

    leaps = lax.switch(roots[0] % 4, [branch(g) for g in range(4)], *blocks)
    steps = [(z - root) % 8 for root in roots]
    held = jnp.stack(
        [
            jnp.where(d == 0, v, jnp.where(d == 3, up, down))
            for d, v, (up, down) in zip(steps, blocks, leaps)
        ]
    )
    after = lax.ppermute(held, "z", [(k, (k + 1) % 8) for k in range(8)])
    before = lax.ppermute(held, "z", [(k, (k - 1) % 8) for k in range(8)])
    whole = []
    for i, d in enumerate(steps):
        from_after = (d == 1) | (d == 4) | (d == 6)
        from_before = (d == 2) | (d == 7)
        whole.append(
            jnp.where(from_after, after[i], jnp.where(from_before, before[i], held[i]))
        )
    return whole


def strips(spectra, panels):
    flat = spectra.reshape(2 * FREQ, ROWS, COLS)
    lane_panel = lax.broadcasted_iota(jnp.int32, (1, 1, 2 * ROWS), 2) // ROWS
    picked = [
        lax.dynamic_slice_in_dim(flat, (panels[i] % 16) * ROWS, ROWS, 2) for i in range(2)
    ]
    block = jnp.concatenate(picked, axis=2)
    owners = panels // 16
    for axis, bit in (("c", owners % 2), ("yh", owners // 2)):
        other = lax.ppermute(block, axis, [(0, 1), (1, 0)])
        keep = jnp.where(lane_panel == 0, bit[0], bit[1]) == lax.axis_index(axis)
        block = jnp.where(keep, block, other)
    return block.reshape(2, FREQ, ROWS, 2 * ROWS)


def kernel(bins, x_ref, l_ref, coef_ref, *refs):
    block_refs, o_ref = refs[:-1], refs[-1]
    total = [None] * TWIN
    for i in range(4):
        own, partner = block_refs[2 * i], block_refs[2 * i + 1]
        cols = own.shape[-1]
        b = jnp.concatenate(
            [own[...].reshape(2 * ROWS, cols), partner[...].reshape(2 * ROWS, cols)], axis=0
        )
        high = b.astype(jnp.bfloat16)
        low = (b - high.astype(jnp.float32)).astype(jnp.bfloat16)
        left = l_ref[bins[i]]
        left_high = left.astype(jnp.bfloat16)
        left_low = (left - left_high.astype(jnp.float32)).astype(jnp.bfloat16)
        product = (
            jnp.dot(left_low, high, preferred_element_type=jnp.float32)
            + jnp.dot(left_high, low, preferred_element_type=jnp.float32)
            + jnp.dot(left_high, high, preferred_element_type=jnp.float32)
        )
        f = bins[i]
        real = x_ref[0, f] - product[:ROWS]
        imag = x_ref[1, f] - product[ROWS:]
        for u in range(TWIN):
            at = u * 8 + i * 2
            term = real * coef_ref[:, at : at + 1] - imag * coef_ref[:, at + 1 : at + 2]
            total[u] = term if total[u] is None else total[u] + term
    for u in range(TWIN):
        o_ref[u] = total[u].astype(o_ref.dtype)


def synthesise(bins, spectra, left, coefs, blocks):
    width = 256
    block_spec = pl.BlockSpec((2, ROWS, width), lambda j, bins: (0, 0, j))
    grid_spec = pltpu.PrefetchScalarGridSpec(
        num_scalar_prefetch=1,
        grid=(COLS // width,),
        in_specs=[
            pl.BlockSpec((2, FREQ, ROWS, width), lambda j, bins: (0, 0, 0, j)),
            pl.BlockSpec((4, 128, 256), lambda j, bins: (0, 0, 0)),
            pl.BlockSpec((ROWS, 64), lambda j, bins: (0, 0)),
            *[block_spec] * 8,
        ],
        out_specs=pl.BlockSpec((TWIN, ROWS, width), lambda j, bins: (0, 0, j)),
    )
    return pl.pallas_call(
        kernel,
        grid_spec=grid_spec,
        out_shape=jax.ShapeDtypeStruct((TWIN, ROWS, COLS), jnp.bfloat16),
        compiler_params=pltpu.CompilerParams(vmem_limit_bytes=40 * 1024 * 1024),
        cost_estimate=pl.CostEstimate(
            flops=2 * 3 * 4 * 128 * 256 * COLS, bytes_accessed=8 * 2**20, transcendentals=0
        ),
    )(bins, spectra, left, coefs, *blocks)


def tables(filters, offsets, strip, bins, yl):
    lag = np.arange(64, dtype=np.int64)[:, None] * (FIRST_BIN + np.arange(FREQ))[None, :] % NT
    lag_angle = lag * (2.0 * math.pi / NT)
    response_cos = jnp.dot(filters, jnp.asarray(np.cos(lag_angle), jnp.float32), precision=HI)
    response_sin = jnp.dot(filters, jnp.asarray(np.sin(lag_angle), jnp.float32), precision=HI)
    a_real, a_imag = strip[0], strip[1]
    rc, rs = response_cos.T[:, :, None], response_sin.T[:, :, None]
    real = a_real * rc + a_imag * rs
    imag = a_imag * rc - a_real * rs
    re_first = jnp.concatenate([real, -imag], axis=2)
    im_first = jnp.concatenate([imag, real], axis=2)
    re_last = jnp.concatenate([-imag, real], axis=2)
    im_last = jnp.concatenate([real, imag], axis=2)
    left = jnp.where(
        yl == 0,
        jnp.concatenate([re_first, im_first], axis=1),
        jnp.concatenate([re_last, im_last], axis=1),
    )
    times = offsets[:, None] + jnp.arange(TWIN, dtype=jnp.int32)[None, :]
    phase = times[:, :, None] * (FIRST_BIN + bins)[None, None, :] % NT
    angle = phase.astype(jnp.float32) * (2.0 * math.pi / NT)
    coefs = jnp.stack([jnp.cos(angle), jnp.sin(angle)], axis=3).reshape(ROWS, 64)
    return left, coefs


def shards(spectra, panels, filters, offsets):
    x, z, yl = lax.axis_index("x"), lax.axis_index("z"), lax.axis_index("yl")
    strip = strips(spectra, panels)
    slot = jnp.where(panels[0] == LAST, 0, 1)
    other = jnp.where(panels[0] == LAST, panels[1], panels[0])
    members = [(f - 2 * c) % 4 * 2 + c for c in range(2) for f in range(4)]
    flat = spectra.reshape(2 * FREQ, ROWS, COLS)
    arrived = lax.all_to_all(
        flat, ("x", "yl"), 0, 0, axis_index_groups=[members], tiled=True
    )
    ox, oz, oy = place_of(other)
    lx, lz, ly = place_of(LAST)
    mine = lax.dynamic_index_in_dim(arrived, oy * 4 + (ox + 2 * oy) % 4, 0, keepdims=False)
    last = arrived[ly * 4 + (lx + 2 * ly) % 4]

    mine, last = line_broadcast((mine, last), (oz, lz), z)
    own = jnp.where(slot == 0, jnp.stack([last, mine]), jnp.stack([mine, last]))
    plane = [(i, j) for i in range(4) for j in range(2)]
    across = [(i * 2 + j, ((i + 2) % 4) * 2 + 1 - j) for i, j in plane]
    partner = lax.ppermute(own, ("x", "yl"), across)
    blocks = [own, partner]
    turn = [(i, (i + 1) % 4) for i in range(4)]
    back = [(i, (i - 1) % 4) for i in range(4)]
    for axis, pairs in (("yl", [(0, 1), (1, 0)]), ("x", turn), ("x", back)):
        for v in (own, partner):
            blocks.append(lax.ppermute(v, axis, pairs))
    blocks[2], blocks[3] = blocks[3], blocks[2]
    mine_bin = (x + 2 * yl) % 4
    bins = (mine_bin + jnp.array([0, 2, 3, 1], jnp.int32)) % 4
    left, coefs = tables(filters, offsets, strip, bins, yl)
    return synthesise(bins, spectra, left, coefs, blocks)


def solution(mesh):
    fine = Mesh(mesh.devices.reshape(4, 8, 2, 2, 2), ("x", "z", "yl", "yh", "c"))
    src, rcv = ("x", "z", "yl"), ("yh", "c")
    return jax.shard_map(
        shards,
        mesh=fine,
        in_specs=(P(None, None, src, rcv), P(), P(src, None), P(src)),
        out_specs=P(None, src, rcv),
        check_vma=False,
    )
```

```python
import math

import jax
import jax.numpy as jnp
import numpy as np
from jax import lax
from jax.experimental import pallas as pl
from jax.experimental.pallas import tpu as pltpu
from jax.sharding import Mesh
from jax.sharding import PartitionSpec as P

TWIN = 8
NT = 2048
FIRST_BIN = 64
FREQ = 4
ROWS = 64
COLS = 1024
WIDTH = 256
PARTS = 2
LAST = 63
HI = lax.Precision.HIGHEST


def place_of(panel):
    return panel // 16, (panel // 2) % 8, panel % 2


def leap(v, group):
    roots = (group, group + 4)
    up = lax.ppermute(v, "z", [(r, (r + 3) % 8) for r in roots])
    down = lax.ppermute(v, "z", [(r, (r - 3) % 8) for r in roots])
    return up, down


def leaps(blocks, roots, z):
    def branch(group):
        return lambda a, b: (leap(a, group), leap(b, LAST // 2 % 4))

    leapt = lax.switch(roots[0] % 4, [branch(g) for g in range(4)], *blocks)
    return jnp.stack(
        [
            jnp.where(d == 0, v, jnp.where(d == 3, up, down))
            for d, v, (up, down) in zip([(z - r) % 8 for r in roots], blocks, leapt)
        ]
    )


def steps(held, roots, z):
    after = lax.ppermute(held, "z", [(k, (k + 1) % 8) for k in range(8)])
    before = lax.ppermute(held, "z", [(k, (k - 1) % 8) for k in range(8)])
    whole = []
    for i, d in enumerate([(z - r) % 8 for r in roots]):
        from_after = (d == 1) | (d == 4) | (d == 6)
        from_before = (d == 2) | (d == 7)
        whole.append(
            jnp.where(from_after, after[i], jnp.where(from_before, before[i], held[i]))
        )
    return whole


def strips(spectra, panels):
    flat = spectra.reshape(2 * FREQ, ROWS, COLS)
    lane_panel = lax.broadcasted_iota(jnp.int32, (1, 1, 2 * ROWS), 2) // ROWS
    picked = [
        lax.dynamic_slice_in_dim(flat, (panels[i] % 16) * ROWS, ROWS, 2) for i in range(2)
    ]
    block = jnp.concatenate(picked, axis=2)
    owners = panels // 16
    for axis, bit in (("c", owners % 2), ("yh", owners // 2)):
        other = lax.ppermute(block, axis, [(0, 1), (1, 0)])
        keep = jnp.where(lane_panel == 0, bit[0], bit[1]) == lax.axis_index(axis)
        block = jnp.where(keep, block, other)
    return block.reshape(2, FREQ, ROWS, 2 * ROWS)


def kernel(bins, x_ref, l_ref, coef_ref, *refs):
    block_refs, o_ref = refs[:8], refs[-1]
    total = [None] * TWIN
    for i in range(4):
        own, partner = block_refs[2 * i], block_refs[2 * i + 1]
        cols = own.shape[-1]
        b = jnp.concatenate(
            [own[...].reshape(2 * ROWS, cols), partner[...].reshape(2 * ROWS, cols)], axis=0
        )
        high = b.astype(jnp.bfloat16)
        low = (b - high.astype(jnp.float32)).astype(jnp.bfloat16)
        left = l_ref[bins[i]]
        left_high = left.astype(jnp.bfloat16)
        left_low = (left - left_high.astype(jnp.float32)).astype(jnp.bfloat16)
        product = (
            jnp.dot(left_low, high, preferred_element_type=jnp.float32)
            + jnp.dot(left_high, low, preferred_element_type=jnp.float32)
            + jnp.dot(left_high, high, preferred_element_type=jnp.float32)
        )
        f = bins[i]
        real = x_ref[0, f] - product[:ROWS]
        imag = x_ref[1, f] - product[ROWS:]
        for u in range(TWIN):
            at = u * 8 + i * 2
            term = real * coef_ref[:, at : at + 1] - imag * coef_ref[:, at + 1 : at + 2]
            total[u] = term if total[u] is None else total[u] + term
    for u in range(TWIN):
        o_ref[u] = total[u].astype(o_ref.dtype)


def synthesise(bins, spectra, left, coefs, blocks, first, count, before=None):
    block_spec = pl.BlockSpec((2, ROWS, WIDTH), lambda j, bins: (0, 0, j))
    in_specs = [
        pl.BlockSpec((2, FREQ, ROWS, WIDTH), lambda j, bins: (0, 0, 0, first + j)),
        pl.BlockSpec((4, 128, 256), lambda j, bins: (0, 0, 0)),
        pl.BlockSpec((ROWS, 64), lambda j, bins: (0, 0)),
        *[block_spec] * 8,
    ]
    operands = [bins, spectra, left, coefs, *blocks]
    aliases = {}
    if before is not None:
        in_specs.append(pl.BlockSpec(memory_space=pl.ANY))
        operands.append(before)
        aliases = {len(operands) - 1: 0}
    grid_spec = pltpu.PrefetchScalarGridSpec(
        num_scalar_prefetch=1,
        grid=(count,),
        in_specs=in_specs,
        out_specs=pl.BlockSpec((TWIN, ROWS, WIDTH), lambda j, bins: (0, 0, first + j)),
    )
    return pl.pallas_call(
        kernel,
        grid_spec=grid_spec,
        out_shape=jax.ShapeDtypeStruct((TWIN, ROWS, COLS), jnp.bfloat16),
        input_output_aliases=aliases,
        compiler_params=pltpu.CompilerParams(vmem_limit_bytes=40 * 1024 * 1024),
        cost_estimate=pl.CostEstimate(
            flops=2 * 3 * 4 * 128 * 256 * WIDTH * count,
            bytes_accessed=2 * 2**20 * count,
            transcendentals=0,
        ),
    )(*operands)


def tables(filters, offsets, strip, bins, yl):
    lag = np.arange(64, dtype=np.int64)[:, None] * (FIRST_BIN + np.arange(FREQ))[None, :] % NT
    lag_angle = lag * (2.0 * math.pi / NT)
    response_cos = jnp.dot(filters, jnp.asarray(np.cos(lag_angle), jnp.float32), precision=HI)
    response_sin = jnp.dot(filters, jnp.asarray(np.sin(lag_angle), jnp.float32), precision=HI)
    a_real, a_imag = strip[0], strip[1]
    rc, rs = response_cos.T[:, :, None], response_sin.T[:, :, None]
    real = a_real * rc + a_imag * rs
    imag = a_imag * rc - a_real * rs
    re_first = jnp.concatenate([real, -imag], axis=2)
    im_first = jnp.concatenate([imag, real], axis=2)
    re_last = jnp.concatenate([-imag, real], axis=2)
    im_last = jnp.concatenate([real, imag], axis=2)
    left = jnp.where(
        yl == 0,
        jnp.concatenate([re_first, im_first], axis=1),
        jnp.concatenate([re_last, im_last], axis=1),
    )
    times = offsets[:, None] + jnp.arange(TWIN, dtype=jnp.int32)[None, :]
    phase = times[:, :, None] * (FIRST_BIN + bins)[None, None, :] % NT
    angle = phase.astype(jnp.float32) * (2.0 * math.pi / NT)
    coefs = jnp.stack([jnp.cos(angle), jnp.sin(angle)], axis=3).reshape(ROWS, 64)
    return left, coefs


def scatter(rows):
    members = [(f - 2 * c) % 4 * 2 + c for c in range(2) for f in range(4)]
    return lax.all_to_all(rows, ("x", "yl"), 0, 0, axis_index_groups=[members], tiled=True)


def exchange(own):
    plane = [(i, j) for i in range(4) for j in range(2)]
    across = [(i * 2 + j, ((i + 2) % 4) * 2 + 1 - j) for i, j in plane]
    partner = lax.ppermute(own, ("x", "yl"), across)
    blocks = [own, partner]
    turn = [(i, (i + 1) % 4) for i in range(4)]
    back = [(i, (i - 1) % 4) for i in range(4)]
    for axis, pairs in (("yl", [(0, 1), (1, 0)]), ("x", turn), ("x", back)):
        for v in (own, partner):
            blocks.append(lax.ppermute(v, axis, pairs))
    blocks[2], blocks[3] = blocks[3], blocks[2]
    return blocks


def shards(spectra, panels, filters, offsets):
    x, z, yl = lax.axis_index("x"), lax.axis_index("z"), lax.axis_index("yl")
    slot = jnp.where(panels[0] == LAST, 0, 1)
    other = jnp.where(panels[0] == LAST, panels[1], panels[0])
    ox, oz, oy = place_of(other)
    lx, lz, ly = place_of(LAST)
    flat = spectra.reshape(2 * FREQ, ROWS, COLS)
    strip = strips(spectra, panels)
    bins = ((x + 2 * yl) % 4 + jnp.array([0, 2, 3, 1], jnp.int32)) % 4
    half = COLS // PARTS
    owns, held = [], None
    for part in range(PARTS):
        arrived = scatter(flat[:, :, part * half : (part + 1) * half])
        if part:
            held, arrived = lax.optimization_barrier((held, arrived))
            owns.append(steps(held, (oz, lz), z))
        mine = lax.dynamic_index_in_dim(arrived, oy * 4 + (ox + 2 * oy) % 4, 0, keepdims=False)
        last = arrived[ly * 4 + (lx + 2 * ly) % 4]
        held = leaps((mine, last), (oz, lz), z)
    owns.append(steps(held, (oz, lz), z))
    owns = [jnp.where(slot == 0, jnp.stack([b, a]), jnp.stack([a, b])) for a, b in owns]
    owns[0], strip = lax.optimization_barrier((owns[0], strip))
    left, coefs = tables(filters, offsets, strip, bins, yl)
    result = None
    for part in range(PARTS):
        count = half // WIDTH
        result = synthesise(
            bins, spectra, left, coefs, exchange(owns[part]), part * count, count, result
        )
    return result


def solution(mesh):
    fine = Mesh(mesh.devices.reshape(4, 8, 2, 2, 2), ("x", "z", "yl", "yh", "c"))
    src, rcv = ("x", "z", "yl"), ("yh", "c")
    return jax.shard_map(
        shards,
        mesh=fine,
        in_specs=(P(None, None, src, rcv), P(), P(src, None), P(src)),
        out_specs=P(None, src, rcv),
        check_vma=False,
    )
```

```python
import math

import jax
import jax.numpy as jnp
import numpy as np
from jax import lax
from jax.experimental import pallas as pl
from jax.experimental.pallas import tpu as pltpu
from jax.sharding import Mesh
from jax.sharding import PartitionSpec as P

TWIN = 8
NT = 2048
FIRST_BIN = 64
FREQ = 4
ROWS = 64
COLS = 1024
WIDTH = 256
PARTS = 2
LAST = 63
HI = lax.Precision.HIGHEST


def place_of(panel):
    return panel >> 4, (panel >> 1) & 7, panel & 1


def leap(v, groups):
    roots = [g + k for g in groups for k in (0, 4)]
    up = lax.ppermute(v, "z", [(r, (r + 3) % 8) for r in roots])
    down = lax.ppermute(v, "z", [(r, (r - 3) % 8) for r in roots])
    return up, down


def leaps(mine, last, root, z):
    fixed = LAST // 2 % 4

    def branch(group):
        def both(a, b):
            up, down = leap(jnp.where(z & 3 == fixed, b, a), (group, fixed))
            return up, down, up, down

        def apart(a, b):
            return (*leap(a, (fixed,)), *leap(b, (fixed,)))

        return apart if group == fixed else both

    leapt = lax.switch(root & 3, [branch(g) for g in range(4)], mine, last)
    held = []
    for i, (v, d) in enumerate(((mine, (z - root) & 7), (last, (z - LAST // 2 % 8) & 7))):
        up, down = leapt[2 * i], leapt[2 * i + 1]
        held.append(jnp.where(d == 0, v, jnp.where(d == 3, up, down)))
    return jnp.stack(held)


def steps(held, roots, z):
    after = lax.ppermute(held, "z", [(k, (k + 1) % 8) for k in range(8)])
    before = lax.ppermute(held, "z", [(k, (k - 1) % 8) for k in range(8)])
    whole = []
    for i, d in enumerate([(z - r) & 7 for r in roots]):
        from_after = (d == 1) | (d == 4) | (d == 6)
        from_before = (d == 2) | (d == 7)
        whole.append(
            jnp.where(from_after, after[i], jnp.where(from_before, before[i], held[i]))
        )
    return whole


def strips(spectra, panels):
    flat = spectra.reshape(2 * FREQ, ROWS, COLS)
    lane_panel = lax.broadcasted_iota(jnp.int32, (1, 1, 2 * ROWS), 2) // ROWS
    picked = [
        lax.dynamic_slice_in_dim(flat, (panels[i].astype(jnp.uint32) & 15) * ROWS, ROWS, 2)
        for i in range(2)
    ]
    block = jnp.concatenate(picked, axis=2)
    owners = panels >> 4
    for axis, bit in (("c", owners & 1), ("yh", owners >> 1)):
        other = lax.ppermute(block, axis, [(0, 1), (1, 0)])
        keep = jnp.where(lane_panel == 0, bit[0], bit[1]) == lax.axis_index(axis)
        block = jnp.where(keep, block, other)
    return block.reshape(2, FREQ, ROWS, 2 * ROWS)


def kernel(bins, x_ref, l_ref, coef_ref, *refs):
    block_refs, o_ref = refs[:8], refs[-1]
    total = [None] * TWIN
    for i in range(4):
        own, partner = block_refs[2 * i], block_refs[2 * i + 1]
        cols = own.shape[-1]
        b = jnp.concatenate(
            [own[...].reshape(2 * ROWS, cols), partner[...].reshape(2 * ROWS, cols)], axis=0
        )
        high = b.astype(jnp.bfloat16)
        low = (b - high.astype(jnp.float32)).astype(jnp.bfloat16)
        left = l_ref[bins[i]]
        left_high = left.astype(jnp.bfloat16)
        left_low = (left - left_high.astype(jnp.float32)).astype(jnp.bfloat16)
        product = (
            jnp.dot(left_low, high, preferred_element_type=jnp.float32)
            + jnp.dot(left_high, low, preferred_element_type=jnp.float32)
            + jnp.dot(left_high, high, preferred_element_type=jnp.float32)
        )
        f = bins[i]
        real = x_ref[0, f] - product[:ROWS]
        imag = x_ref[1, f] - product[ROWS:]
        for u in range(TWIN):
            at = u * 8 + i * 2
            term = real * coef_ref[:, at : at + 1] - imag * coef_ref[:, at + 1 : at + 2]
            total[u] = term if total[u] is None else total[u] + term
    for u in range(TWIN):
        o_ref[u] = total[u].astype(o_ref.dtype)


def synthesise(bins, spectra, left, coefs, blocks, first, count, before=None):
    block_spec = pl.BlockSpec((2, ROWS, WIDTH), lambda j, bins: (0, 0, j))
    in_specs = [
        pl.BlockSpec((2, FREQ, ROWS, WIDTH), lambda j, bins: (0, 0, 0, first + j)),
        pl.BlockSpec((4, 128, 256), lambda j, bins: (0, 0, 0)),
        pl.BlockSpec((ROWS, 64), lambda j, bins: (0, 0)),
        *[block_spec] * 8,
    ]
    operands = [bins, spectra, left, coefs, *blocks]
    aliases = {}
    if before is not None:
        in_specs.append(pl.BlockSpec(memory_space=pl.ANY))
        operands.append(before)
        aliases = {len(operands) - 1: 0}
    grid_spec = pltpu.PrefetchScalarGridSpec(
        num_scalar_prefetch=1,
        grid=(count,),
        in_specs=in_specs,
        out_specs=pl.BlockSpec((TWIN, ROWS, WIDTH), lambda j, bins: (0, 0, first + j)),
    )
    return pl.pallas_call(
        kernel,
        grid_spec=grid_spec,
        out_shape=jax.ShapeDtypeStruct((TWIN, ROWS, COLS), jnp.bfloat16),
        input_output_aliases=aliases,
        compiler_params=pltpu.CompilerParams(vmem_limit_bytes=40 * 1024 * 1024),
        cost_estimate=pl.CostEstimate(
            flops=2 * 3 * 4 * 128 * 256 * WIDTH * count,
            bytes_accessed=2 * 2**20 * count,
            transcendentals=0,
        ),
    )(*operands)


def tables(filters, offsets, strip, bins, yl):
    lag = np.arange(64, dtype=np.int64)[:, None] * (FIRST_BIN + np.arange(FREQ))[None, :] % NT
    lag_angle = lag * (2.0 * math.pi / NT)
    response_cos = jnp.dot(filters, jnp.asarray(np.cos(lag_angle), jnp.float32), precision=HI)
    response_sin = jnp.dot(filters, jnp.asarray(np.sin(lag_angle), jnp.float32), precision=HI)
    a_real, a_imag = strip[0], strip[1]
    rc, rs = response_cos.T[:, :, None], response_sin.T[:, :, None]
    real = a_real * rc + a_imag * rs
    imag = a_imag * rc - a_real * rs
    re_first = jnp.concatenate([real, -imag], axis=2)
    im_first = jnp.concatenate([imag, real], axis=2)
    re_last = jnp.concatenate([-imag, real], axis=2)
    im_last = jnp.concatenate([real, imag], axis=2)
    left = jnp.where(
        yl == 0,
        jnp.concatenate([re_first, im_first], axis=1),
        jnp.concatenate([re_last, im_last], axis=1),
    )
    times = offsets[:, None] + jnp.arange(TWIN, dtype=jnp.int32)[None, :]
    phase = times[:, :, None] * (FIRST_BIN + bins)[None, None, :] & (NT - 1)
    angle = phase.astype(jnp.float32) * (2.0 * math.pi / NT)
    coefs = jnp.stack([jnp.cos(angle), jnp.sin(angle)], axis=3).reshape(ROWS, 64)
    return left, coefs


def scatter(rows):
    members = [(f - 2 * c) % 4 * 2 + c for c in range(2) for f in range(4)]
    return lax.all_to_all(rows, ("x", "yl"), 0, 0, axis_index_groups=[members], tiled=True)


def exchange(own):
    plane = [(i, j) for i in range(4) for j in range(2)]
    across = [(i * 2 + j, ((i + 2) % 4) * 2 + 1 - j) for i, j in plane]
    partner = lax.ppermute(own, ("x", "yl"), across)
    blocks = [own, partner]
    turn = [(i, (i + 1) % 4) for i in range(4)]
    back = [(i, (i - 1) % 4) for i in range(4)]
    for axis, pairs in (("yl", [(0, 1), (1, 0)]), ("x", turn), ("x", back)):
        for v in (own, partner):
            blocks.append(lax.ppermute(v, axis, pairs))
    blocks[2], blocks[3] = blocks[3], blocks[2]
    return blocks


def shards(spectra, panels, filters, offsets):
    x, z, yl = lax.axis_index("x"), lax.axis_index("z"), lax.axis_index("yl")
    slot = jnp.where(panels[0] == LAST, 0, 1)
    other = jnp.where(panels[0] == LAST, panels[1], panels[0])
    ox, oz, oy = place_of(other)
    lx, lz, ly = place_of(LAST)
    half = COLS // PARTS
    later, pieces = spectra, []
    for part in range(PARTS):
        flat = later.reshape(2 * FREQ, ROWS, COLS)
        later, piece = lax.optimization_barrier(
            (later, flat[:, :, part * half : (part + 1) * half])
        )
        pieces.append(piece)
    strip = strips(later, panels)
    bins = (x + 2 * yl + jnp.array([0, 2, 3, 1], jnp.int32)) & 3
    spot = (oy * 4 + ((ox + 2 * oy) & 3)).astype(jnp.uint32)
    owns, held = [], None
    for part in range(PARTS):
        arrived = scatter(pieces[part])
        if part:
            held, arrived = lax.optimization_barrier((held, arrived))
            owns.append(steps(held, (oz, lz), z))
        mine = lax.dynamic_index_in_dim(arrived, spot, 0, keepdims=False)
        last = arrived[ly * 4 + (lx + 2 * ly) % 4]
        held = leaps(mine, last, oz, z)
    owns.append(steps(held, (oz, lz), z))
    owns = [jnp.where(slot == 0, jnp.stack([b, a]), jnp.stack([a, b])) for a, b in owns]
    owns[0], strip = lax.optimization_barrier((owns[0], strip))
    left, coefs = tables(filters, offsets, strip, bins, yl)
    result = None
    for part in range(PARTS):
        count = half // WIDTH
        result = synthesise(
            bins, spectra, left, coefs, exchange(owns[part]), part * count, count, result
        )
    return result


def solution(mesh):
    fine = Mesh(mesh.devices.reshape(4, 8, 2, 2, 2), ("x", "z", "yl", "yh", "c"))
    src, rcv = ("x", "z", "yl"), ("yh", "c")
    return jax.shard_map(
        shards,
        mesh=fine,
        in_specs=(P(None, None, src, rcv), P(), P(src, None), P(src)),
        out_specs=P(None, src, rcv),
        check_vma=False,
    )
```

```python
import math

import jax
import jax.numpy as jnp
import numpy as np
from jax import lax
from jax.experimental import pallas as pl
from jax.experimental.pallas import tpu as pltpu
from jax.sharding import Mesh
from jax.sharding import PartitionSpec as P

TWIN = 8
NT = 2048
FIRST_BIN = 64
FREQ = 4
ROWS = 64
COLS = 1024
WIDTH = 256
LAST = 63
HI = lax.Precision.HIGHEST


def place_of(panel):
    return panel >> 4, (panel >> 1) & 7, panel & 1


def leap(v, roots):
    up = lax.ppermute(v, "z", [(r, (r + 3) % 8) for r in roots])
    down = lax.ppermute(v, "z", [(r, (r - 3) % 8) for r in roots])
    return up, down


def leaps(mine, last, root, z):
    fixed = place_of(LAST)[1]

    def both(group):
        roots = [group, group + 4] + ([3, 7] if group != 3 else [])

        def branch(a, b):
            spare = jnp.zeros_like(a)
            return (*leap(jnp.where(z == fixed, b, a), roots), spare, spare + 1)

        return branch

    def apart(a, b):
        return (*leap(a, [3, 7]), *leap(b, [3, 7]))

    case = jnp.where(root == fixed, 4, root & 3)
    up, down, last_up, last_down = lax.switch(
        case, [both(0), both(1), both(2), both(3), apart], mine, last
    )
    d, e = (z - root) & 7, (z - fixed) & 7
    mine = jnp.where(d == 0, mine, jnp.where(d == 3, up, down))
    last_up = jnp.where(root == fixed, last_up, up)
    last_down = jnp.where(root == fixed, last_down, down)
    last = jnp.where(e == 0, last, jnp.where(e == 3, last_up, last_down))
    return mine, last


def steps(held, root, z):
    after = lax.ppermute(held, "z", [(k, (k + 1) % 8) for k in range(8)])
    before = lax.ppermute(held, "z", [(k, (k - 1) % 8) for k in range(8)])
    d = (z - root) & 7
    from_after = (d == 1) | (d == 4) | (d == 6)
    from_before = (d == 2) | (d == 7)
    return jnp.where(from_after, after, jnp.where(from_before, before, held))


def strips(spectra, panel):
    flat = spectra.reshape(2 * FREQ, ROWS, COLS)
    is_first = lax.broadcasted_iota(jnp.int32, (1, 1, 2 * ROWS), 2) < ROWS
    start = (panel.astype(jnp.uint32) & 15) * ROWS
    block = jnp.concatenate(
        [lax.dynamic_slice_in_dim(flat, start, ROWS, 2), flat[:, :, COLS - ROWS :]], axis=2
    )
    owner = panel >> 4
    for axis, bit in (("c", owner & 1), ("yh", owner >> 1)):
        other = lax.ppermute(block, axis, [(0, 1), (1, 0)])
        keep = jnp.where(is_first, bit, 1) == lax.axis_index(axis)
        block = jnp.where(keep, block, other)
    return block.reshape(2, FREQ, ROWS, 2 * ROWS)


def kernel(bins, x_ref, l_ref, coef_ref, *refs):
    block_refs, o_ref = refs[:16], refs[16]
    total = [None] * TWIN
    for i in range(4):
        b = jnp.concatenate([r[...] for r in block_refs[4 * i : 4 * i + 4]], axis=0)
        high = b.astype(jnp.bfloat16)
        low = (b - high.astype(jnp.float32)).astype(jnp.bfloat16)
        f = bins[i]
        left = l_ref[f]
        left_high = left.astype(jnp.bfloat16)
        left_low = (left - left_high.astype(jnp.float32)).astype(jnp.bfloat16)
        both = jnp.dot(
            jnp.concatenate([left_high, left_low], axis=0),
            high,
            preferred_element_type=jnp.float32,
        )
        rest = jnp.dot(left_high, low, preferred_element_type=jnp.float32)
        product = both[: 2 * ROWS] + (both[2 * ROWS :] + rest)
        real = x_ref[0, f] - product[:ROWS]
        imag = x_ref[1, f] - product[ROWS:]
        for u in range(TWIN):
            at = u * 8 + i * 2
            term = real * coef_ref[:, at : at + 1] - imag * coef_ref[:, at + 1 : at + 2]
            total[u] = term if total[u] is None else total[u] + term
    for u in range(TWIN):
        o_ref[u] = total[u].astype(o_ref.dtype)


def synthesise(bins, spectra, left, coefs, blocks):
    grid_spec = pltpu.PrefetchScalarGridSpec(
        num_scalar_prefetch=1,
        grid=(COLS // WIDTH,),
        in_specs=[
            pl.BlockSpec((2, FREQ, ROWS, WIDTH), lambda j, bins: (0, 0, 0, j)),
            pl.BlockSpec((4, 128, 256), lambda j, bins: (0, 0, 0)),
            pl.BlockSpec((ROWS, 64), lambda j, bins: (0, 0)),
            *[pl.BlockSpec((ROWS, WIDTH), lambda j, bins: (0, j))] * 16,
        ],
        out_specs=pl.BlockSpec((TWIN, ROWS, WIDTH), lambda j, bins: (0, 0, j)),
    )
    return pl.pallas_call(
        kernel,
        grid_spec=grid_spec,
        out_shape=jax.ShapeDtypeStruct((TWIN, ROWS, COLS), jnp.bfloat16),
        compiler_params=pltpu.CompilerParams(vmem_limit_bytes=40 * 1024 * 1024),
        cost_estimate=pl.CostEstimate(
            flops=2 * 3 * 4 * 128 * 256 * COLS, bytes_accessed=8 * 2**20, transcendentals=0
        ),
    )(bins, spectra, left, coefs, *blocks)


def tables(filters, offsets, strip, bins, yl):
    lag = np.arange(64, dtype=np.int64)[:, None] * (FIRST_BIN + np.arange(FREQ))[None, :] % NT
    lag_angle = lag * (2.0 * math.pi / NT)
    response_cos = jnp.dot(filters, jnp.asarray(np.cos(lag_angle), jnp.float32), precision=HI)
    response_sin = jnp.dot(filters, jnp.asarray(np.sin(lag_angle), jnp.float32), precision=HI)
    a_real, a_imag = strip[0], strip[1]
    rc, rs = response_cos.T[:, :, None], response_sin.T[:, :, None]
    real = a_real * rc + a_imag * rs
    imag = a_imag * rc - a_real * rs
    re_first = jnp.concatenate([real, -imag], axis=2)
    im_first = jnp.concatenate([imag, real], axis=2)
    re_last = jnp.concatenate([-imag, real], axis=2)
    im_last = jnp.concatenate([real, imag], axis=2)
    left = jnp.where(
        yl == 0,
        jnp.concatenate([re_first, im_first], axis=1),
        jnp.concatenate([re_last, im_last], axis=1),
    )
    times = offsets[:, None] + jnp.arange(TWIN, dtype=jnp.int32)[None, :]
    phase = times[:, :, None] * (FIRST_BIN + bins)[None, None, :] & (NT - 1)
    angle = phase.astype(jnp.float32) * (2.0 * math.pi / NT)
    coefs = jnp.stack([jnp.cos(angle), jnp.sin(angle)], axis=3).reshape(ROWS, 64)
    return left, coefs


def scatter(rows):
    members = [(f - 2 * c) % 4 * 2 + c for c in range(2) for f in range(4)]
    return lax.all_to_all(rows, ("x", "yl"), 0, 0, axis_index_groups=[members], tiled=True)


def exchange(own):
    plane = [(i, j) for i in range(4) for j in range(2)]
    across = [(i * 2 + j, ((i + 2) % 4) * 2 + 1 - j) for i, j in plane]
    partner = lax.ppermute(own, ("x", "yl"), across)
    blocks = [own, partner]
    turn = [(i, (i + 1) % 4) for i in range(4)]
    back = [(i, (i - 1) % 4) for i in range(4)]
    for axis, pairs in (("yl", [(0, 1), (1, 0)]), ("x", turn), ("x", back)):
        for v in (own, partner):
            blocks.append(lax.ppermute(v, axis, pairs))
    blocks[2], blocks[3] = blocks[3], blocks[2]
    return blocks


def shards(spectra, panels, filters, offsets):
    x, z, yl = lax.axis_index("x"), lax.axis_index("z"), lax.axis_index("yl")
    other_first = panels[1] == LAST
    other = jnp.where(other_first, panels[0], panels[1])
    ox, oz, oy = place_of(other)
    lx, lz, ly = place_of(LAST)
    strip = strips(spectra, other)
    arrived = scatter(spectra.reshape(2 * FREQ, ROWS, COLS))
    arrived, strip = lax.optimization_barrier((arrived, strip))
    spot = (oy * 4 + ((ox + 2 * oy) & 3)).astype(jnp.uint32)
    mine = lax.dynamic_index_in_dim(arrived, spot, 0, keepdims=False)
    last = arrived[ly * 4 + (lx + 2 * ly) % 4]
    mine, last = leaps(mine, last, oz, z)
    last = exchange(steps(last, lz, z))
    mine = exchange(steps(mine, oz, z))
    blocks = [v for pair in zip(mine, last) for v in pair]
    bins = (x + 2 * yl + jnp.array([0, 2, 3, 1], jnp.int32)) & 3
    left, coefs = tables(filters, offsets, strip, bins, yl)
    return synthesise(bins, spectra, left, coefs, blocks)


def solution(mesh):
    fine = Mesh(mesh.devices.reshape(4, 8, 2, 2, 2), ("x", "z", "yl", "yh", "c"))
    src, rcv = ("x", "z", "yl"), ("yh", "c")
    return jax.shard_map(
        shards,
        mesh=fine,
        in_specs=(P(None, None, src, rcv), P(), P(src, None), P(src)),
        out_specs=P(None, src, rcv),
        check_vma=False,
    )
```

```python
import math

import jax
import jax.numpy as jnp
import numpy as np
from jax import lax
from jax.experimental import pallas as pl
from jax.experimental.pallas import tpu as pltpu
from jax.sharding import Mesh
from jax.sharding import PartitionSpec as P

TWIN = 8
NT = 2048
FIRST_BIN = 64
FREQ = 4
ROWS = 64
COLS = 1024
WIDTH = 256
LAST = 63
HI = lax.Precision.HIGHEST


def place_of(panel):
    return panel >> 4, (panel >> 1) & 7, panel & 1


def leap(v, root):
    up = lax.ppermute(v, "z", [(root, (root + 3) % 8)])
    down = lax.ppermute(v, "z", [(root, (root - 3) % 8)])
    return up, down


def land(v, leapt, root, z):
    d = (z - root) & 7
    return jnp.where(d == 0, v, jnp.where(d == 3, leapt[0], leapt[1]))


def steps(held, root, z):
    after = lax.ppermute(held, "z", [(k, (k + 1) % 8) for k in range(8)])
    before = lax.ppermute(held, "z", [(k, (k - 1) % 8) for k in range(8)])
    d = (z - root) & 7
    from_after = (d == 1) | (d == 4) | (d == 6)
    from_before = (d == 2) | (d == 7)
    return jnp.where(from_after, after, jnp.where(from_before, before, held))


def strips(spectra, panel):
    flat = spectra.reshape(2 * FREQ, ROWS, COLS)
    is_first = lax.broadcasted_iota(jnp.int32, (1, 1, 2 * ROWS), 2) < ROWS
    start = (panel.astype(jnp.uint32) & 15) * ROWS
    block = jnp.concatenate(
        [lax.dynamic_slice_in_dim(flat, start, ROWS, 2), flat[:, :, COLS - ROWS :]], axis=2
    )
    owner = panel >> 4
    for axis, bit in (("c", owner & 1), ("yh", owner >> 1)):
        other = lax.ppermute(block, axis, [(0, 1), (1, 0)])
        keep = jnp.where(is_first, bit, 1) == lax.axis_index(axis)
        block = jnp.where(keep, block, other)
    return block.reshape(2, FREQ, ROWS, 2 * ROWS)


def kernel(bins, x_ref, l_ref, coef_ref, *refs):
    block_refs, o_ref = refs[:16], refs[16]
    total = [None] * TWIN
    for i in range(4):
        b = jnp.concatenate([r[...] for r in block_refs[4 * i : 4 * i + 4]], axis=0)
        high = b.astype(jnp.bfloat16)
        low = (b - high.astype(jnp.float32)).astype(jnp.bfloat16)
        f = bins[i]
        left = l_ref[f]
        left_high = left.astype(jnp.bfloat16)
        left_low = (left - left_high.astype(jnp.float32)).astype(jnp.bfloat16)
        both = jnp.dot(
            jnp.concatenate([left_high, left_low], axis=0),
            high,
            preferred_element_type=jnp.float32,
        )
        rest = jnp.dot(left_high, low, preferred_element_type=jnp.float32)
        product = both[: 2 * ROWS] + (both[2 * ROWS :] + rest)
        real = x_ref[0, f] - product[:ROWS]
        imag = x_ref[1, f] - product[ROWS:]
        for u in range(TWIN):
            at = u * 8 + i * 2
            term = real * coef_ref[:, at : at + 1] - imag * coef_ref[:, at + 1 : at + 2]
            total[u] = term if total[u] is None else total[u] + term
    for u in range(TWIN):
        o_ref[u] = total[u].astype(o_ref.dtype)


def synthesise(bins, spectra, left, coefs, blocks):
    grid_spec = pltpu.PrefetchScalarGridSpec(
        num_scalar_prefetch=1,
        grid=(COLS // WIDTH,),
        in_specs=[
            pl.BlockSpec((2, FREQ, ROWS, WIDTH), lambda j, bins: (0, 0, 0, j)),
            pl.BlockSpec((4, 128, 256), lambda j, bins: (0, 0, 0)),
            pl.BlockSpec((ROWS, 64), lambda j, bins: (0, 0)),
            *[pl.BlockSpec((ROWS, WIDTH), lambda j, bins: (0, j))] * 16,
        ],
        out_specs=pl.BlockSpec((TWIN, ROWS, WIDTH), lambda j, bins: (0, 0, j)),
    )
    return pl.pallas_call(
        kernel,
        grid_spec=grid_spec,
        out_shape=jax.ShapeDtypeStruct((TWIN, ROWS, COLS), jnp.bfloat16),
        compiler_params=pltpu.CompilerParams(vmem_limit_bytes=40 * 1024 * 1024),
        cost_estimate=pl.CostEstimate(
            flops=2 * 3 * 4 * 128 * 256 * COLS, bytes_accessed=8 * 2**20, transcendentals=0
        ),
    )(bins, spectra, left, coefs, *blocks)


def tables(filters, offsets, strip, bins, yl):
    lag = np.arange(64, dtype=np.int64)[:, None] * (FIRST_BIN + np.arange(FREQ))[None, :] % NT
    lag_angle = lag * (2.0 * math.pi / NT)
    response_cos = jnp.dot(filters, jnp.asarray(np.cos(lag_angle), jnp.float32), precision=HI)
    response_sin = jnp.dot(filters, jnp.asarray(np.sin(lag_angle), jnp.float32), precision=HI)
    a_real, a_imag = strip[0], strip[1]
    rc, rs = response_cos.T[:, :, None], response_sin.T[:, :, None]
    real = a_real * rc + a_imag * rs
    imag = a_imag * rc - a_real * rs
    re_first = jnp.concatenate([real, -imag], axis=2)
    im_first = jnp.concatenate([imag, real], axis=2)
    re_last = jnp.concatenate([-imag, real], axis=2)
    im_last = jnp.concatenate([real, imag], axis=2)
    left = jnp.where(
        yl == 0,
        jnp.concatenate([re_first, im_first], axis=1),
        jnp.concatenate([re_last, im_last], axis=1),
    )
    times = offsets[:, None] + jnp.arange(TWIN, dtype=jnp.int32)[None, :]
    phase = times[:, :, None] * (FIRST_BIN + bins)[None, None, :] & (NT - 1)
    angle = phase.astype(jnp.float32) * (2.0 * math.pi / NT)
    coefs = jnp.stack([jnp.cos(angle), jnp.sin(angle)], axis=3).reshape(ROWS, 64)
    return left, coefs


def scatter(rows):
    members = [(f - 2 * c) % 4 * 2 + c for c in range(2) for f in range(4)]
    return lax.all_to_all(rows, ("x", "yl"), 0, 0, axis_index_groups=[members], tiled=True)


def exchange(own):
    plane = [(i, j) for i in range(4) for j in range(2)]
    across = [(i * 2 + j, ((i + 2) % 4) * 2 + 1 - j) for i, j in plane]
    partner = lax.ppermute(own, ("x", "yl"), across)
    blocks = [own, partner]
    turn = [(i, (i + 1) % 4) for i in range(4)]
    back = [(i, (i - 1) % 4) for i in range(4)]
    for axis, pairs in (("yl", [(0, 1), (1, 0)]), ("x", turn), ("x", back)):
        for v in (own, partner):
            blocks.append(lax.ppermute(v, axis, pairs))
    blocks[2], blocks[3] = blocks[3], blocks[2]
    return blocks


def shards(spectra, panels, filters, offsets):
    x, z, yl = lax.axis_index("x"), lax.axis_index("z"), lax.axis_index("yl")
    other_first = panels[1] == LAST
    other = jnp.where(other_first, panels[0], panels[1])
    ox, oz, oy = place_of(other)
    lx, lz, ly = place_of(LAST)
    strip = strips(spectra, other)
    arrived = scatter(spectra.reshape(2 * FREQ, ROWS, COLS))
    spot = (oy * 4 + ((ox + 2 * oy) & 3)).astype(jnp.uint32)
    mine = lax.dynamic_index_in_dim(arrived, spot, 0, keepdims=False)
    last = arrived[ly * 4 + (lx + 2 * ly) % 4]
    last = land(last, leap(last, lz), lz, z)
    branches = [lambda v, r=r: leap(v, r) for r in range(8)]
    mine = land(mine, lax.switch(oz, branches, mine), oz, z)
    last, strip = lax.optimization_barrier((steps(last, lz, z), strip))
    last = exchange(last)
    mine = exchange(steps(mine, oz, z))
    blocks = [v for pair in zip(mine, last) for v in pair]
    bins = (x + 2 * yl + jnp.array([0, 2, 3, 1], jnp.int32)) & 3
    left, coefs = tables(filters, offsets, strip, bins, yl)
    return synthesise(bins, spectra, left, coefs, blocks)


def solution(mesh):
    fine = Mesh(mesh.devices.reshape(4, 8, 2, 2, 2), ("x", "z", "yl", "yh", "c"))
    src, rcv = ("x", "z", "yl"), ("yh", "c")
    return jax.shard_map(
        shards,
        mesh=fine,
        in_specs=(P(None, None, src, rcv), P(), P(src, None), P(src)),
        out_specs=P(None, src, rcv),
        check_vma=False,
    )
```

```python
import math

import jax
import jax.numpy as jnp
import numpy as np
from jax import lax
from jax.experimental import pallas as pl
from jax.experimental.pallas import tpu as pltpu
from jax.sharding import Mesh
from jax.sharding import PartitionSpec as P

TWIN = 8
NT = 2048
FIRST_BIN = 64
FREQ = 4
ROWS = 64
COLS = 1024
WIDTH = 256
LAST = 63
HI = lax.Precision.HIGHEST


def place_of(panel):
    return panel >> 4, (panel >> 1) & 7, panel & 1


def leap(v, root):
    up = lax.ppermute(v, "z", [(root, (root + 3) % 8)])
    down = lax.ppermute(v, "z", [(root, (root - 3) % 8)])
    return up, down


def land(v, leapt, root, z):
    d = (z - root) & 7
    return jnp.where(d == 0, v, jnp.where(d == 3, leapt[0], leapt[1]))


def steps(held, root, z):
    after = lax.ppermute(held, "z", [(k, (k + 1) % 8) for k in range(8)])
    before = lax.ppermute(held, "z", [(k, (k - 1) % 8) for k in range(8)])
    d = (z - root) & 7
    from_after = (d == 1) | (d == 4) | (d == 6)
    from_before = (d == 2) | (d == 7)
    return jnp.where(from_after, after, jnp.where(from_before, before, held))


def strips(spectra, panel):
    flat = spectra.reshape(2 * FREQ, ROWS, COLS)
    start = (panel.astype(jnp.uint32) & 15) * ROWS
    block = jnp.concatenate(
        [lax.dynamic_slice_in_dim(flat, start, ROWS, 2), flat[:, :, COLS - ROWS :]], axis=2
    )
    return block


def swap(block, panel, axis):
    is_first = lax.broadcasted_iota(jnp.int32, (1, 1, 2 * ROWS), 2) < ROWS
    bit = panel >> 4 & 1 if axis == "c" else panel >> 5
    other = lax.ppermute(block, axis, [(0, 1), (1, 0)])
    keep = jnp.where(is_first, bit, 1) == lax.axis_index(axis)
    return jnp.where(keep, block, other)


def kernel(bins, x_ref, l_ref, coef_ref, *refs):
    block_refs, o_ref = refs[:16], refs[16]
    total = [None] * TWIN
    for i in range(4):
        b = jnp.concatenate([r[...] for r in block_refs[4 * i : 4 * i + 4]], axis=0)
        high = b.astype(jnp.bfloat16)
        low = (b - high.astype(jnp.float32)).astype(jnp.bfloat16)
        f = bins[i]
        left = l_ref[f]
        left_high = left.astype(jnp.bfloat16)
        left_low = (left - left_high.astype(jnp.float32)).astype(jnp.bfloat16)
        both = jnp.dot(
            jnp.concatenate([left_high, left_low], axis=0),
            high,
            preferred_element_type=jnp.float32,
        )
        rest = jnp.dot(left_high, low, preferred_element_type=jnp.float32)
        product = both[: 2 * ROWS] + (both[2 * ROWS :] + rest)
        real = x_ref[0, f] - product[:ROWS]
        imag = x_ref[1, f] - product[ROWS:]
        for u in range(TWIN):
            at = u * 8 + i * 2
            term = real * coef_ref[:, at : at + 1] - imag * coef_ref[:, at + 1 : at + 2]
            total[u] = term if total[u] is None else total[u] + term
    for u in range(TWIN):
        o_ref[u] = total[u].astype(o_ref.dtype)


def synthesise(bins, spectra, left, coefs, blocks):
    grid_spec = pltpu.PrefetchScalarGridSpec(
        num_scalar_prefetch=1,
        grid=(COLS // WIDTH,),
        in_specs=[
            pl.BlockSpec((2, FREQ, ROWS, WIDTH), lambda j, bins: (0, 0, 0, j)),
            pl.BlockSpec((4, 128, 256), lambda j, bins: (0, 0, 0)),
            pl.BlockSpec((ROWS, 64), lambda j, bins: (0, 0)),
            *[pl.BlockSpec((ROWS, WIDTH), lambda j, bins: (0, j))] * 16,
        ],
        out_specs=pl.BlockSpec((TWIN, ROWS, WIDTH), lambda j, bins: (0, 0, j)),
    )
    return pl.pallas_call(
        kernel,
        grid_spec=grid_spec,
        out_shape=jax.ShapeDtypeStruct((TWIN, ROWS, COLS), jnp.bfloat16),
        compiler_params=pltpu.CompilerParams(vmem_limit_bytes=40 * 1024 * 1024),
        cost_estimate=pl.CostEstimate(
            flops=2 * 3 * 4 * 128 * 256 * COLS, bytes_accessed=8 * 2**20, transcendentals=0
        ),
    )(bins, spectra, left, coefs, *blocks)


def tables(filters, offsets, strip, bins, yl):
    lag = np.arange(64, dtype=np.int64)[:, None] * (FIRST_BIN + np.arange(FREQ))[None, :] % NT
    lag_angle = lag * (2.0 * math.pi / NT)
    response_cos = jnp.dot(filters, jnp.asarray(np.cos(lag_angle), jnp.float32), precision=HI)
    response_sin = jnp.dot(filters, jnp.asarray(np.sin(lag_angle), jnp.float32), precision=HI)
    a_real, a_imag = strip[0], strip[1]
    rc, rs = response_cos.T[:, :, None], response_sin.T[:, :, None]
    real = a_real * rc + a_imag * rs
    imag = a_imag * rc - a_real * rs
    re_first = jnp.concatenate([real, -imag], axis=2)
    im_first = jnp.concatenate([imag, real], axis=2)
    re_last = jnp.concatenate([-imag, real], axis=2)
    im_last = jnp.concatenate([real, imag], axis=2)
    left = jnp.where(
        yl == 0,
        jnp.concatenate([re_first, im_first], axis=1),
        jnp.concatenate([re_last, im_last], axis=1),
    )
    times = offsets[:, None] + jnp.arange(TWIN, dtype=jnp.int32)[None, :]
    phase = times[:, :, None] * (FIRST_BIN + bins)[None, None, :] & (NT - 1)
    angle = phase.astype(jnp.float32) * (2.0 * math.pi / NT)
    coefs = jnp.stack([jnp.cos(angle), jnp.sin(angle)], axis=3).reshape(ROWS, 64)
    return left, coefs


def scatter(rows):
    members = [(f - 2 * c) % 4 * 2 + c for c in range(2) for f in range(4)]
    return lax.all_to_all(rows, ("x", "yl"), 0, 0, axis_index_groups=[members], tiled=True)


def exchange(panels):
    def send(v, way):
        axis, pairs = {
            "on": ("x", [(i, (i + 1) % 4) for i in range(4)]),
            "back": ("x", [(i, (i - 1) % 4) for i in range(4)]),
            "y": ("yl", [(0, 1), (1, 0)]),
        }[way]
        return lax.ppermute(v, axis, pairs)

    near = [(send(own, "on"), send(own, "back"), send(own, "y")) for own in panels]
    mid = [(send(a, "on"), send(c, "back"), send(a, "y")) for a, _, c in near]
    far = [
        send(d, "y") if i == 0 else send(e, "back") for i, (d, e, _) in enumerate(mid)
    ]
    return [
        [own, g, d, c, a, e, b, f]
        for own, (a, b, c), (d, e, f), g in zip(panels, near, mid, far)
    ]


def shards(spectra, panels, filters, offsets):
    x, z, yl = lax.axis_index("x"), lax.axis_index("z"), lax.axis_index("yl")
    other_first = panels[1] == LAST
    other = jnp.where(other_first, panels[0], panels[1])
    ox, oz, oy = place_of(other)
    lx, lz, ly = place_of(LAST)
    strip = swap(strips(spectra, other), other, "c")
    arrived = scatter(spectra.reshape(2 * FREQ, ROWS, COLS))
    arrived, strip = lax.optimization_barrier((arrived, strip))
    spot = (oy * 4 + ((ox + 2 * oy) & 3)).astype(jnp.uint32)
    mine = lax.dynamic_index_in_dim(arrived, spot, 0, keepdims=False)
    last = arrived[ly * 4 + (lx + 2 * ly) % 4]
    last = land(last, leap(last, lz), lz, z)
    branches = [lambda v, r=r: leap(v, r) for r in range(8)]
    mine = land(mine, lax.switch(oz, branches, mine), oz, z)
    mine, strip = lax.optimization_barrier((mine, strip))
    strip = swap(strip, other, "yh").reshape(2, FREQ, ROWS, 2 * ROWS)
    last, mine = exchange([steps(last, lz, z), steps(mine, oz, z)])
    blocks = [v for pair in zip(mine, last) for v in pair]
    bins = (x + 2 * yl + jnp.array([0, 2, 3, 1], jnp.int32)) & 3
    left, coefs = tables(filters, offsets, strip, bins, yl)
    return synthesise(bins, spectra, left, coefs, blocks)


def solution(mesh):
    fine = Mesh(mesh.devices.reshape(4, 8, 2, 2, 2), ("x", "z", "yl", "yh", "c"))
    src, rcv = ("x", "z", "yl"), ("yh", "c")
    return jax.shard_map(
        shards,
        mesh=fine,
        in_specs=(P(None, None, src, rcv), P(), P(src, None), P(src)),
        out_specs=P(None, src, rcv),
        check_vma=False,
    )
```

```python
import math

import jax
import jax.numpy as jnp
import numpy as np
from jax import lax
from jax.experimental import pallas as pl
from jax.experimental.pallas import tpu as pltpu
from jax.sharding import Mesh
from jax.sharding import PartitionSpec as P

TWIN = 8
NT = 2048
FIRST_BIN = 64
FREQ = 4
ROWS = 64
COLS = 1024
WIDTH = 256
LAST = 63
HI = lax.Precision.HIGHEST


def place_of(panel):
    return panel >> 4, (panel >> 1) & 7, panel & 1


def leap(v, root):
    up = lax.ppermute(v, "z", [(root, (root + 3) % 8)])
    down = lax.ppermute(v, "z", [(root, (root - 3) % 8)])
    return up, down


def land(v, leapt, root, z):
    d = (z - root) & 7
    return jnp.where(d == 0, v, jnp.where(d == 3, leapt[0], leapt[1]))


def steps(held, root, z):
    after = lax.ppermute(held, "z", [(k, (k + 1) % 8) for k in range(8)])
    before = lax.ppermute(held, "z", [(k, (k - 1) % 8) for k in range(8)])
    d = (z - root) & 7
    from_after = (d == 1) | (d == 4) | (d == 6)
    from_before = (d == 2) | (d == 7)
    return jnp.where(from_after, after, jnp.where(from_before, before, held))


def strips(spectra, panel):
    flat = spectra.reshape(2 * FREQ, ROWS, COLS)
    start = (panel.astype(jnp.uint32) & 15) * ROWS
    block = jnp.concatenate(
        [lax.dynamic_slice_in_dim(flat, start, ROWS, 2), flat[:, :, COLS - ROWS :]], axis=2
    )
    return block


def swap(block, panel, axis):
    is_first = lax.broadcasted_iota(jnp.int32, (1, 1, 2 * ROWS), 2) < ROWS
    bit = panel >> 4 & 1 if axis == "c" else panel >> 5
    other = lax.ppermute(block, axis, [(0, 1), (1, 0)])
    keep = jnp.where(is_first, bit, 1) == lax.axis_index(axis)
    return jnp.where(keep, block, other)


def kernel(bins, x_ref, l_ref, coef_ref, *refs):
    block_refs, o_ref = refs[:16], refs[16]
    total = [None] * TWIN
    for i in range(4):
        b = jnp.concatenate([r[...] for r in block_refs[4 * i : 4 * i + 4]], axis=0)
        high = b.astype(jnp.bfloat16)
        low = (b - high.astype(jnp.float32)).astype(jnp.bfloat16)
        f = bins[i]
        left = l_ref[f]
        left_high = left.astype(jnp.bfloat16)
        left_low = (left - left_high.astype(jnp.float32)).astype(jnp.bfloat16)
        both = jnp.dot(
            jnp.concatenate([left_high, left_low], axis=0),
            high,
            preferred_element_type=jnp.float32,
        )
        rest = jnp.dot(left_high, low, preferred_element_type=jnp.float32)
        product = both[: 2 * ROWS] + (both[2 * ROWS :] + rest)
        real = x_ref[0, f] - product[:ROWS]
        imag = x_ref[1, f] - product[ROWS:]
        for u in range(TWIN):
            at = u * 8 + i * 2
            term = real * coef_ref[:, at : at + 1] - imag * coef_ref[:, at + 1 : at + 2]
            total[u] = term if total[u] is None else total[u] + term
    for u in range(TWIN):
        o_ref[u] = total[u].astype(o_ref.dtype)


def synthesise(bins, spectra, left, coefs, blocks):
    grid_spec = pltpu.PrefetchScalarGridSpec(
        num_scalar_prefetch=1,
        grid=(COLS // WIDTH,),
        in_specs=[
            pl.BlockSpec((2, FREQ, ROWS, WIDTH), lambda j, bins: (0, 0, 0, j)),
            pl.BlockSpec((4, 128, 256), lambda j, bins: (0, 0, 0)),
            pl.BlockSpec((ROWS, 64), lambda j, bins: (0, 0)),
            *[pl.BlockSpec((ROWS, WIDTH), lambda j, bins: (0, j))] * 16,
        ],
        out_specs=pl.BlockSpec((TWIN, ROWS, WIDTH), lambda j, bins: (0, 0, j)),
    )
    return pl.pallas_call(
        kernel,
        grid_spec=grid_spec,
        out_shape=jax.ShapeDtypeStruct((TWIN, ROWS, COLS), jnp.bfloat16),
        compiler_params=pltpu.CompilerParams(vmem_limit_bytes=40 * 1024 * 1024),
        cost_estimate=pl.CostEstimate(
            flops=2 * 3 * 4 * 128 * 256 * COLS, bytes_accessed=8 * 2**20, transcendentals=0
        ),
    )(bins, spectra, left, coefs, *blocks)


def tables(filters, offsets, strip, bins, yl):
    lag = np.arange(64, dtype=np.int64)[:, None] * (FIRST_BIN + np.arange(FREQ))[None, :] % NT
    lag_angle = lag * (2.0 * math.pi / NT)
    response_cos = jnp.dot(filters, jnp.asarray(np.cos(lag_angle), jnp.float32), precision=HI)
    response_sin = jnp.dot(filters, jnp.asarray(np.sin(lag_angle), jnp.float32), precision=HI)
    a_real, a_imag = strip[0], strip[1]
    rc, rs = response_cos.T[:, :, None], response_sin.T[:, :, None]
    real = a_real * rc + a_imag * rs
    imag = a_imag * rc - a_real * rs
    re_first = jnp.concatenate([real, -imag], axis=2)
    im_first = jnp.concatenate([imag, real], axis=2)
    re_last = jnp.concatenate([-imag, real], axis=2)
    im_last = jnp.concatenate([real, imag], axis=2)
    left = jnp.where(
        yl == 0,
        jnp.concatenate([re_first, im_first], axis=1),
        jnp.concatenate([re_last, im_last], axis=1),
    )
    times = offsets[:, None] + jnp.arange(TWIN, dtype=jnp.int32)[None, :]
    phase = times[:, :, None] * (FIRST_BIN + bins)[None, None, :] & (NT - 1)
    angle = phase.astype(jnp.float32) * (2.0 * math.pi / NT)
    coefs = jnp.stack([jnp.cos(angle), jnp.sin(angle)], axis=3).reshape(ROWS, 64)
    return left, coefs


def scatter(rows):
    members = [(f - 2 * c) % 4 * 2 + c for c in range(2) for f in range(4)]
    return lax.all_to_all(rows, ("x", "yl"), 0, 0, axis_index_groups=[members], tiled=True)


def exchange(panels):
    def send(v, way):
        axis, pairs = {
            "on": ("x", [(i, (i + 1) % 4) for i in range(4)]),
            "back": ("x", [(i, (i - 1) % 4) for i in range(4)]),
            "y": ("yl", [(0, 1), (1, 0)]),
        }[way]
        return lax.ppermute(v, axis, pairs)

    near = [(send(own, "on"), send(own, "back"), send(own, "y")) for own in panels]
    mid = [(send(a, "on"), send(c, "back"), send(a, "y")) for a, _, c in near]
    far = [
        send(d, "y") if i == 0 else send(e, "back") for i, (d, e, _) in enumerate(mid)
    ]
    return [
        [own, g, d, c, a, e, b, f]
        for own, (a, b, c), (d, e, f), g in zip(panels, near, mid, far)
    ]


def shards(spectra, panels, filters, offsets):
    x, z, yl = lax.axis_index("x"), lax.axis_index("z"), lax.axis_index("yl")
    other_first = panels[1] == LAST
    other = jnp.where(other_first, panels[0], panels[1])
    ox, oz, oy = place_of(other)
    lx, lz, ly = place_of(LAST)
    strip = swap(strips(spectra, other), other, "c")
    arrived = scatter(spectra.reshape(2 * FREQ, ROWS, COLS))
    arrived, strip = lax.optimization_barrier((arrived, strip))
    spot = (oy * 4 + ((ox + 2 * oy) & 3)).astype(jnp.uint32)
    mine = lax.dynamic_index_in_dim(arrived, spot, 0, keepdims=False)
    last = arrived[ly * 4 + (lx + 2 * ly) % 4]
    bins = (x + 2 * yl + jnp.array([0, 2, 3, 1], jnp.int32)) & 3

    def rest(root):
        def run(mine, last, strip):
            last = land(last, leap(last, lz), lz, z)
            mine = land(mine, leap(mine, root), root, z)
            mine, strip = lax.optimization_barrier((mine, strip))
            strip = swap(strip, other, "yh").reshape(2, FREQ, ROWS, 2 * ROWS)
            last, mine = exchange([steps(last, lz, z), steps(mine, root, z)])
            blocks = [v for pair in zip(mine, last) for v in pair]
            left, coefs = tables(filters, offsets, strip, bins, yl)
            return synthesise(bins, spectra, left, coefs, blocks)

        return run

    return lax.switch(oz, [rest(r) for r in range(8)], mine, last, strip)


def solution(mesh):
    fine = Mesh(mesh.devices.reshape(4, 8, 2, 2, 2), ("x", "z", "yl", "yh", "c"))
    src, rcv = ("x", "z", "yl"), ("yh", "c")
    return jax.shard_map(
        shards,
        mesh=fine,
        in_specs=(P(None, None, src, rcv), P(), P(src, None), P(src)),
        out_specs=P(None, src, rcv),
        check_vma=False,
    )
```

```python
import math

import jax
import jax.numpy as jnp
import numpy as np
from jax import lax
from jax.experimental import pallas as pl
from jax.experimental.pallas import tpu as pltpu
from jax.sharding import Mesh
from jax.sharding import PartitionSpec as P

TWIN = 8
NT = 2048
FIRST_BIN = 64
FREQ = 4
ROWS = 64
COLS = 1024
GROUP = 16
LAST = 63
HI = lax.Precision.HIGHEST


def place_of(panel):
    return panel >> 4, (panel >> 1) & 7, panel & 1


def leap(v, root):
    up = lax.ppermute(v, "z", [(root, (root + 3) % 8)])
    down = lax.ppermute(v, "z", [(root, (root - 3) % 8)])
    return up, down


def land(v, leapt, root, z):
    d = (z - root) & 7
    return jnp.where(d == 0, v, jnp.where(d == 3, leapt[0], leapt[1]))


def steps(held, root, z):
    after = lax.ppermute(held, "z", [(k, (k + 1) % 8) for k in range(8)])
    before = lax.ppermute(held, "z", [(k, (k - 1) % 8) for k in range(8)])
    d = (z - root) & 7
    from_after = (d == 1) | (d == 4) | (d == 6)
    from_before = (d == 2) | (d == 7)
    return jnp.where(from_after, after, jnp.where(from_before, before, held))


def strips(spectra, panel):
    flat = spectra.reshape(2 * FREQ, ROWS, COLS)
    start = (panel.astype(jnp.uint32) & 15) * ROWS
    block = jnp.concatenate(
        [lax.dynamic_slice_in_dim(flat, start, ROWS, 2), flat[:, :, COLS - ROWS :]], axis=2
    )
    return block


def swap(block, panel, axis):
    is_first = lax.broadcasted_iota(jnp.int32, (1, 1, 2 * ROWS), 2) < ROWS
    bit = panel >> 4 & 1 if axis == "c" else panel >> 5
    other = lax.ppermute(block, axis, [(0, 1), (1, 0)])
    keep = jnp.where(is_first, bit, 1) == lax.axis_index(axis)
    return jnp.where(keep, block, other)


def partial(sets, bins, x_ref, l_ref, coef_ref, block_refs, before_ref, d_ref, store):
    for n, i in enumerate(sets):
        b = jnp.concatenate([r[...] for r in block_refs[4 * n : 4 * n + 4]], axis=0)
        high = b.astype(jnp.bfloat16)
        low = (b - high.astype(jnp.float32)).astype(jnp.bfloat16)
        f = bins[i]
        left = l_ref[f]
        left_high = left.astype(jnp.bfloat16)
        left_low = (left - left_high.astype(jnp.float32)).astype(jnp.bfloat16)
        both = jnp.dot(
            jnp.concatenate([left_high, left_low], axis=0),
            high,
            preferred_element_type=jnp.float32,
        )
        rest = jnp.dot(left_high, low, preferred_element_type=jnp.float32)
        product = both[: 2 * ROWS] + (both[2 * ROWS :] + rest)
        d_ref[2 * n] = x_ref[0, f] - product[:ROWS]
        d_ref[2 * n + 1] = x_ref[1, f] - product[ROWS:]
    for first in range(0, ROWS, GROUP):
        rows = slice(first, first + GROUP)
        spectrum = [d_ref[k, rows, :] for k in range(2 * len(sets))]
        for u in range(TWIN):
            total = None if before_ref is None else before_ref[u, rows, :]
            for k, value in enumerate(spectrum):
                at = u * 8 + 2 * sets[0] + k
                term = value * coef_ref[rows, at : at + 1]
                total = term if total is None else total + term
            store(u, rows, total)


def early_kernel(bins, x_ref, l_ref, coef_ref, *refs):
    block_refs, o_ref, d_ref = refs[:12], refs[12], refs[13]

    def store(u, rows, total):
        o_ref[u, rows, :] = total

    partial((1, 2, 3), bins, x_ref, l_ref, coef_ref, block_refs, None, d_ref, store)


def late_kernel(bins, x_ref, l_ref, coef_ref, *refs):
    block_refs, before_ref, o_ref, d_ref = refs[:4], refs[4], refs[5], refs[6]

    def store(u, rows, total):
        o_ref[u, rows, :] = total.astype(o_ref.dtype)

    partial((0,), bins, x_ref, l_ref, coef_ref, block_refs, before_ref, d_ref, store)


def synthesise(bins, spectra, left, coefs, blocks):
    vmem = pl.BlockSpec(memory_space=pltpu.VMEM)

    def call(body, sets, dtype, operands):
        return pl.pallas_call(
            body,
            in_specs=[pl.BlockSpec(memory_space=pltpu.SMEM), *[vmem] * len(operands)],
            out_specs=vmem,
            out_shape=jax.ShapeDtypeStruct((TWIN, ROWS, COLS), dtype),
            scratch_shapes=[pltpu.VMEM((2 * sets, ROWS, COLS), jnp.float32)],
            compiler_params=pltpu.CompilerParams(vmem_limit_bytes=24 * 1024 * 1024),
            cost_estimate=pl.CostEstimate(
                flops=2 * 3 * sets * 128 * 256 * COLS,
                bytes_accessed=2 * 2**20 * sets,
                transcendentals=0,
            ),
        )(bins, *operands)

    early = call(early_kernel, 3, jnp.float32, [spectra, left, coefs, *blocks[4:]])
    return call(
        late_kernel, 1, jnp.bfloat16, [spectra, left, coefs, *blocks[:4], early]
    )


def tables(filters, offsets, strip, bins, yl):
    lag = np.arange(64, dtype=np.int64)[:, None] * (FIRST_BIN + np.arange(FREQ))[None, :] % NT
    lag_angle = lag * (2.0 * math.pi / NT)
    response_cos = jnp.dot(filters, jnp.asarray(np.cos(lag_angle), jnp.float32), precision=HI)
    response_sin = jnp.dot(filters, jnp.asarray(np.sin(lag_angle), jnp.float32), precision=HI)
    a_real, a_imag = strip[0], strip[1]
    rc, rs = response_cos.T[:, :, None], response_sin.T[:, :, None]
    real = a_real * rc + a_imag * rs
    imag = a_imag * rc - a_real * rs
    re_first = jnp.concatenate([real, -imag], axis=2)
    im_first = jnp.concatenate([imag, real], axis=2)
    re_last = jnp.concatenate([-imag, real], axis=2)
    im_last = jnp.concatenate([real, imag], axis=2)
    left = jnp.where(
        yl == 0,
        jnp.concatenate([re_first, im_first], axis=1),
        jnp.concatenate([re_last, im_last], axis=1),
    )
    times = offsets[:, None] + jnp.arange(TWIN, dtype=jnp.int32)[None, :]
    phase = times[:, :, None] * (FIRST_BIN + bins)[None, None, :] & (NT - 1)
    angle = phase.astype(jnp.float32) * (2.0 * math.pi / NT)
    coefs = jnp.stack([jnp.cos(angle), -jnp.sin(angle)], axis=3).reshape(ROWS, 64)
    return left, coefs


def scatter(rows):
    members = [(f - 2 * c) % 4 * 2 + c for c in range(2) for f in range(4)]
    return lax.all_to_all(rows, ("x", "yl"), 0, 0, axis_index_groups=[members], tiled=True)


def exchange(panels):
    def send(v, way):
        axis, pairs = {
            "on": ("x", [(i, (i + 1) % 4) for i in range(4)]),
            "back": ("x", [(i, (i - 1) % 4) for i in range(4)]),
            "y": ("yl", [(0, 1), (1, 0)]),
        }[way]
        return lax.ppermute(v, axis, pairs)

    near = [(send(own, "on"), send(own, "back"), send(own, "y")) for own in panels]
    mid = [(send(a, "on"), send(c, "back"), send(a, "y")) for a, _, c in near]
    far = [
        send(d, "y") if i == 0 else send(e, "back") for i, (d, e, _) in enumerate(mid)
    ]
    return [
        [own, g, d, c, a, e, b, f]
        for own, (a, b, c), (d, e, f), g in zip(panels, near, mid, far)
    ]


def shards(spectra, panels, filters, offsets):
    x, z, yl = lax.axis_index("x"), lax.axis_index("z"), lax.axis_index("yl")
    other_first = panels[1] == LAST
    other = jnp.where(other_first, panels[0], panels[1])
    ox, oz, oy = place_of(other)
    lx, lz, ly = place_of(LAST)
    strip = swap(strips(spectra, other), other, "c")
    arrived = scatter(spectra.reshape(2 * FREQ, ROWS, COLS))
    arrived, strip = lax.optimization_barrier((arrived, strip))
    spot = (oy * 4 + ((ox + 2 * oy) & 3)).astype(jnp.uint32)
    mine = lax.dynamic_index_in_dim(arrived, spot, 0, keepdims=False)
    last = arrived[ly * 4 + (lx + 2 * ly) % 4]
    last = land(last, leap(last, lz), lz, z)
    branches = [lambda v, r=r: leap(v, r) for r in range(8)]
    mine = land(mine, lax.switch(oz, branches, mine), oz, z)
    mine, strip = lax.optimization_barrier((mine, strip))
    strip = swap(strip, other, "yh").reshape(2, FREQ, ROWS, 2 * ROWS)
    last, mine = exchange([steps(last, lz, z), steps(mine, oz, z)])
    blocks = [v for pair in zip(mine, last) for v in pair]
    bins = (x + 2 * yl + jnp.array([0, 2, 3, 1], jnp.int32)) & 3
    left, coefs = tables(filters, offsets, strip, bins, yl)
    return synthesise(bins, spectra, left, coefs, blocks)


def solution(mesh):
    fine = Mesh(mesh.devices.reshape(4, 8, 2, 2, 2), ("x", "z", "yl", "yh", "c"))
    src, rcv = ("x", "z", "yl"), ("yh", "c")
    return jax.shard_map(
        shards,
        mesh=fine,
        in_specs=(P(None, None, src, rcv), P(), P(src, None), P(src)),
        out_specs=P(None, src, rcv),
        check_vma=False,
    )
```

```python
import math

import jax
import jax.numpy as jnp
import numpy as np
from jax import lax
from jax.experimental import pallas as pl
from jax.experimental.pallas import tpu as pltpu
from jax.sharding import Mesh
from jax.sharding import PartitionSpec as P

TWIN = 8
NT = 2048
FIRST_BIN = 64
FREQ = 4
ROWS = 64
COLS = 1024
GROUP = 16
LAST = 63
HI = lax.Precision.HIGHEST


def place_of(panel):
    return panel >> 4, (panel >> 1) & 7, panel & 1


def leap(v, root):
    up = lax.ppermute(v, "z", [(root, (root + 3) % 8)])
    down = lax.ppermute(v, "z", [(root, (root - 3) % 8)])
    return up, down


def land(v, leapt, root, z):
    d = (z - root) & 7
    return jnp.where(d == 0, v, jnp.where(d == 3, leapt[0], leapt[1]))


def steps(held, root, z, exact):
    def pairs(step, away):
        senders = [(root + k) % 8 for k in away] if exact else range(8)
        return [(k, (k + step) % 8) for k in senders]

    after = lax.ppermute(held, "z", pairs(1, (0, 3, 5)))
    before = lax.ppermute(held, "z", pairs(-1, (0, 3)))
    d = (z - root) & 7
    from_after = (d == 1) | (d == 4) | (d == 6)
    from_before = (d == 2) | (d == 7)
    return jnp.where(from_after, after, jnp.where(from_before, before, held))


def strips(spectra, panel):
    flat = spectra.reshape(2 * FREQ, ROWS, COLS)
    start = (panel.astype(jnp.uint32) & 15) * ROWS
    block = jnp.concatenate(
        [lax.dynamic_slice_in_dim(flat, start, ROWS, 2), flat[:, :, COLS - ROWS :]], axis=2
    )
    return block


def swap(block, panel, axis):
    is_first = lax.broadcasted_iota(jnp.int32, (1, 1, 2 * ROWS), 2) < ROWS
    bit = panel >> 4 & 1 if axis == "c" else panel >> 5
    other = lax.ppermute(block, axis, [(0, 1), (1, 0)])
    keep = jnp.where(is_first, bit, 1) == lax.axis_index(axis)
    return jnp.where(keep, block, other)


def partial(sets, bins, x_ref, l_ref, coef_ref, block_refs, before_ref, d_ref, store):
    for n, i in enumerate(sets):
        b = jnp.concatenate([r[...] for r in block_refs[4 * n : 4 * n + 4]], axis=0)
        high = b.astype(jnp.bfloat16)
        low = (b - high.astype(jnp.float32)).astype(jnp.bfloat16)
        f = bins[i]
        left = l_ref[f]
        left_high = left.astype(jnp.bfloat16)
        left_low = (left - left_high.astype(jnp.float32)).astype(jnp.bfloat16)
        both = jnp.dot(
            jnp.concatenate([left_high, left_low], axis=0),
            high,
            preferred_element_type=jnp.float32,
        )
        rest = jnp.dot(left_high, low, preferred_element_type=jnp.float32)
        product = both[: 2 * ROWS] + (both[2 * ROWS :] + rest)
        d_ref[2 * n] = x_ref[0, f] - product[:ROWS]
        d_ref[2 * n + 1] = x_ref[1, f] - product[ROWS:]
    for first in range(0, ROWS, GROUP):
        rows = slice(first, first + GROUP)
        spectrum = [d_ref[k, rows, :] for k in range(2 * len(sets))]
        for u in range(TWIN):
            total = None if before_ref is None else before_ref[u, rows, :]
            for k, value in enumerate(spectrum):
                at = u * 8 + 2 * sets[0] + k
                term = value * coef_ref[rows, at : at + 1]
                total = term if total is None else total + term
            store(u, rows, total)


def early_kernel(bins, x_ref, l_ref, coef_ref, *refs):
    block_refs, o_ref, d_ref = refs[:12], refs[12], refs[13]

    def store(u, rows, total):
        o_ref[u, rows, :] = total

    partial((1, 2, 3), bins, x_ref, l_ref, coef_ref, block_refs, None, d_ref, store)


def late_kernel(bins, x_ref, l_ref, coef_ref, *refs):
    block_refs, before_ref, o_ref, d_ref = refs[:4], refs[4], refs[5], refs[6]

    def store(u, rows, total):
        o_ref[u, rows, :] = total.astype(o_ref.dtype)

    partial((0,), bins, x_ref, l_ref, coef_ref, block_refs, before_ref, d_ref, store)


def synthesise(bins, spectra, left, coefs, blocks):
    vmem = pl.BlockSpec(memory_space=pltpu.VMEM)

    def call(body, sets, dtype, operands):
        return pl.pallas_call(
            body,
            in_specs=[pl.BlockSpec(memory_space=pltpu.SMEM), *[vmem] * len(operands)],
            out_specs=vmem,
            out_shape=jax.ShapeDtypeStruct((TWIN, ROWS, COLS), dtype),
            scratch_shapes=[pltpu.VMEM((2 * sets, ROWS, COLS), jnp.float32)],
            compiler_params=pltpu.CompilerParams(vmem_limit_bytes=24 * 1024 * 1024),
            cost_estimate=pl.CostEstimate(
                flops=2 * 3 * sets * 128 * 256 * COLS,
                bytes_accessed=2 * 2**20 * sets,
                transcendentals=0,
            ),
        )(bins, *operands)

    early = call(early_kernel, 3, jnp.float32, [spectra, left, coefs, *blocks[4:]])
    return call(
        late_kernel, 1, jnp.bfloat16, [spectra, left, coefs, *blocks[:4], early]
    )


def tables(filters, offsets, strip, bins, yl):
    lag = np.arange(64, dtype=np.int64)[:, None] * (FIRST_BIN + np.arange(FREQ))[None, :] % NT
    lag_angle = lag * (2.0 * math.pi / NT)
    response_cos = jnp.dot(filters, jnp.asarray(np.cos(lag_angle), jnp.float32), precision=HI)
    response_sin = jnp.dot(filters, jnp.asarray(np.sin(lag_angle), jnp.float32), precision=HI)
    a_real, a_imag = strip[0], strip[1]
    rc, rs = response_cos.T[:, :, None], response_sin.T[:, :, None]
    real = a_real * rc + a_imag * rs
    imag = a_imag * rc - a_real * rs
    re_first = jnp.concatenate([real, -imag], axis=2)
    im_first = jnp.concatenate([imag, real], axis=2)
    re_last = jnp.concatenate([-imag, real], axis=2)
    im_last = jnp.concatenate([real, imag], axis=2)
    left = jnp.where(
        yl == 0,
        jnp.concatenate([re_first, im_first], axis=1),
        jnp.concatenate([re_last, im_last], axis=1),
    )
    times = offsets[:, None] + jnp.arange(TWIN, dtype=jnp.int32)[None, :]
    phase = times[:, :, None] * (FIRST_BIN + bins)[None, None, :] & (NT - 1)
    angle = phase.astype(jnp.float32) * (2.0 * math.pi / NT)
    coefs = jnp.stack([jnp.cos(angle), -jnp.sin(angle)], axis=3).reshape(ROWS, 64)
    return left, coefs


def scatter(rows):
    members = [(f - 2 * c) % 4 * 2 + c for c in range(2) for f in range(4)]
    return lax.all_to_all(rows, ("x", "yl"), 0, 0, axis_index_groups=[members], tiled=True)


def exchange(panels):
    def send(v, way):
        axis, pairs = {
            "on": ("x", [(i, (i + 1) % 4) for i in range(4)]),
            "back": ("x", [(i, (i - 1) % 4) for i in range(4)]),
            "y": ("yl", [(0, 1), (1, 0)]),
        }[way]
        return lax.ppermute(v, axis, pairs)

    near = [(send(own, "on"), send(own, "back"), send(own, "y")) for own in panels]
    mid = [(send(a, "on"), send(c, "back"), send(a, "y")) for a, _, c in near]
    far = [
        send(d, "y") if i == 0 else send(e, "back") for i, (d, e, _) in enumerate(mid)
    ]
    return [
        [own, g, d, c, a, e, b, f]
        for own, (a, b, c), (d, e, f), g in zip(panels, near, mid, far)
    ]


def shards(spectra, panels, filters, offsets):
    x, z, yl = lax.axis_index("x"), lax.axis_index("z"), lax.axis_index("yl")
    other_first = panels[1] == LAST
    other = jnp.where(other_first, panels[0], panels[1])
    ox, oz, oy = place_of(other)
    lx, lz, ly = place_of(LAST)
    strip = swap(strips(spectra, other), other, "c")
    arrived = scatter(spectra.reshape(2 * FREQ, ROWS, COLS))
    arrived, strip = lax.optimization_barrier((arrived, strip))
    spot = (oy * 4 + ((ox + 2 * oy) & 3)).astype(jnp.uint32)
    mine = lax.dynamic_index_in_dim(arrived, spot, 0, keepdims=False)
    last = arrived[ly * 4 + (lx + 2 * ly) % 4]
    last = land(last, leap(last, lz), lz, z)
    branches = [lambda v, r=r: leap(v, r) for r in range(8)]
    mine = land(mine, lax.switch(oz, branches, mine), oz, z)
    mine, strip = lax.optimization_barrier((mine, strip))
    strip = swap(strip, other, "yh").reshape(2, FREQ, ROWS, 2 * ROWS)
    last, mine = exchange([steps(last, lz, z, True), steps(mine, oz, z, False)])
    blocks = [v for pair in zip(mine, last) for v in pair]
    bins = (x + 2 * yl + jnp.array([0, 2, 3, 1], jnp.int32)) & 3
    left, coefs = tables(filters, offsets, strip, bins, yl)
    return synthesise(bins, spectra, left, coefs, blocks)


def solution(mesh):
    fine = Mesh(mesh.devices.reshape(4, 8, 2, 2, 2), ("x", "z", "yl", "yh", "c"))
    src, rcv = ("x", "z", "yl"), ("yh", "c")
    return jax.shard_map(
        shards,
        mesh=fine,
        in_specs=(P(None, None, src, rcv), P(), P(src, None), P(src)),
        out_specs=P(None, src, rcv),
        check_vma=False,
    )
```

```python
import math

import jax
import jax.numpy as jnp
import numpy as np
from jax import lax
from jax.experimental import pallas as pl
from jax.experimental.pallas import tpu as pltpu
from jax.sharding import Mesh
from jax.sharding import PartitionSpec as P

TWIN = 8
NT = 2048
FIRST_BIN = 64
FREQ = 4
ROWS = 64
COLS = 1024
GROUP = 16
LAST = 63
HI = lax.Precision.HIGHEST


def place_of(panel):
    return panel >> 4, (panel >> 1) & 7, panel & 1


def leap(v, root):
    up = lax.ppermute(v, "z", [(root, (root + 3) % 8)])
    down = lax.ppermute(v, "z", [(root, (root - 3) % 8)])
    return up, down


def land(v, leapt, root, z):
    d = (z - root) & 7
    return jnp.where(d == 0, v, jnp.where(d == 3, leapt[0], leapt[1]))


def steps(held, root, z, exact):
    def pairs(step, away):
        senders = [(root + k) % 8 for k in away] if exact else range(8)
        return [(k, (k + step) % 8) for k in senders]

    after = lax.ppermute(held, "z", pairs(1, (0, 3, 5)))
    before = lax.ppermute(held, "z", pairs(-1, (0, 3)))
    d = (z - root) & 7
    from_after = (d == 1) | (d == 4) | (d == 6)
    from_before = (d == 2) | (d == 7)
    return jnp.where(from_after, after, jnp.where(from_before, before, held))


def strips(spectra, panel):
    flat = spectra.reshape(2 * FREQ, ROWS, COLS)
    start = (panel.astype(jnp.uint32) & 15) * ROWS
    block = jnp.concatenate(
        [lax.dynamic_slice_in_dim(flat, start, ROWS, 2), flat[:, :, COLS - ROWS :]], axis=2
    )
    return block


def swap(block, panel, axis):
    is_first = lax.broadcasted_iota(jnp.int32, (1, 1, 2 * ROWS), 2) < ROWS
    bit = panel >> 4 & 1 if axis == "c" else panel >> 5
    other = lax.ppermute(block, axis, [(0, 1), (1, 0)])
    keep = jnp.where(is_first, bit, 1) == lax.axis_index(axis)
    return jnp.where(keep, block, other)


def partial(sets, bins, x_ref, l_ref, coef_ref, block_refs, before_ref, d_ref, store):
    for n, i in enumerate(sets):
        b = jnp.concatenate([r[...] for r in block_refs[4 * n : 4 * n + 4]], axis=0)
        high = b.astype(jnp.bfloat16)
        low = (b - high.astype(jnp.float32)).astype(jnp.bfloat16)
        f = bins[i]
        left = l_ref[f]
        left_high = left.astype(jnp.bfloat16)
        left_low = (left - left_high.astype(jnp.float32)).astype(jnp.bfloat16)
        both = jnp.dot(
            jnp.concatenate([left_high, left_low], axis=0),
            high,
            preferred_element_type=jnp.float32,
        )
        rest = jnp.dot(left_high, low, preferred_element_type=jnp.float32)
        product = both[: 2 * ROWS] + (both[2 * ROWS :] + rest)
        d_ref[2 * n] = x_ref[0, f] - product[:ROWS]
        d_ref[2 * n + 1] = x_ref[1, f] - product[ROWS:]
    for first in range(0, ROWS, GROUP):
        rows = slice(first, first + GROUP)
        spectrum = [d_ref[k, rows, :] for k in range(2 * len(sets))]
        for u in range(TWIN):
            total = None if before_ref is None else before_ref[u, rows, :]
            for k, value in enumerate(spectrum):
                at = u * 8 + 2 * sets[0] + k
                term = value * coef_ref[rows, at : at + 1]
                total = term if total is None else total + term
            store(u, rows, total)


def early_kernel(bins, x_ref, l_ref, coef_ref, *refs):
    block_refs, o_ref, d_ref = refs[:12], refs[12], refs[13]

    def store(u, rows, total):
        o_ref[u, rows, :] = total

    partial((1, 2, 3), bins, x_ref, l_ref, coef_ref, block_refs, None, d_ref, store)


def late_kernel(bins, x_ref, l_ref, coef_ref, *refs):
    block_refs, before_ref, o_ref, d_ref = refs[:4], refs[4], refs[5], refs[6]

    def store(u, rows, total):
        o_ref[u, rows, :] = total.astype(o_ref.dtype)

    partial((0,), bins, x_ref, l_ref, coef_ref, block_refs, before_ref, d_ref, store)


def synthesise(bins, spectra, left, coefs, blocks):
    vmem = pl.BlockSpec(memory_space=pltpu.VMEM)

    def call(body, sets, dtype, operands):
        return pl.pallas_call(
            body,
            in_specs=[pl.BlockSpec(memory_space=pltpu.SMEM), *[vmem] * len(operands)],
            out_specs=vmem,
            out_shape=jax.ShapeDtypeStruct((TWIN, ROWS, COLS), dtype),
            scratch_shapes=[pltpu.VMEM((2 * sets, ROWS, COLS), jnp.float32)],
            compiler_params=pltpu.CompilerParams(vmem_limit_bytes=24 * 1024 * 1024),
            cost_estimate=pl.CostEstimate(
                flops=2 * 3 * sets * 128 * 256 * COLS,
                bytes_accessed=2 * 2**20 * sets,
                transcendentals=0,
            ),
        )(bins, *operands)

    early = call(early_kernel, 3, jnp.float32, [spectra, left, coefs, *blocks[4:]])
    return call(
        late_kernel, 1, jnp.bfloat16, [spectra, left, coefs, *blocks[:4], early]
    )


def tables(filters, offsets, strip, bins, yl):
    lag = np.arange(64, dtype=np.int64)[:, None] * (FIRST_BIN + np.arange(FREQ))[None, :] % NT
    lag_angle = lag * (2.0 * math.pi / NT)
    response_cos = jnp.dot(filters, jnp.asarray(np.cos(lag_angle), jnp.float32), precision=HI)
    response_sin = jnp.dot(filters, jnp.asarray(np.sin(lag_angle), jnp.float32), precision=HI)
    a_real, a_imag = strip[0], strip[1]
    rc, rs = response_cos.T[:, :, None], response_sin.T[:, :, None]
    real = a_real * rc + a_imag * rs
    imag = a_imag * rc - a_real * rs
    re_first = jnp.concatenate([real, -imag], axis=2)
    im_first = jnp.concatenate([imag, real], axis=2)
    re_last = jnp.concatenate([-imag, real], axis=2)
    im_last = jnp.concatenate([real, imag], axis=2)
    left = jnp.where(
        yl == 0,
        jnp.concatenate([re_first, im_first], axis=1),
        jnp.concatenate([re_last, im_last], axis=1),
    )
    times = offsets[:, None] + jnp.arange(TWIN, dtype=jnp.int32)[None, :]
    phase = times[:, :, None] * (FIRST_BIN + bins)[None, None, :] & (NT - 1)
    angle = phase.astype(jnp.float32) * (2.0 * math.pi / NT)
    coefs = jnp.stack([jnp.cos(angle), -jnp.sin(angle)], axis=3).reshape(ROWS, 64)
    return left, coefs


def scatter(rows):
    members = [(f - 2 * c) % 4 * 2 + c for c in range(2) for f in range(4)]
    return lax.all_to_all(rows, ("x", "yl"), 0, 0, axis_index_groups=[members], tiled=True)


def exchange(panels):
    def send(v, way):
        axis, pairs = {
            "on": ("x", [(i, (i + 1) % 4) for i in range(4)]),
            "back": ("x", [(i, (i - 1) % 4) for i in range(4)]),
            "y": ("yl", [(0, 1), (1, 0)]),
        }[way]
        return lax.ppermute(v, axis, pairs)

    near = [(send(own, "on"), send(own, "back"), send(own, "y")) for own in panels]
    mid = [(send(a, "on"), send(c, "back"), send(a, "y")) for a, _, c in near]
    far = [
        send(d, "y") if i == 0 else send(e, "back") for i, (d, e, _) in enumerate(mid)
    ]
    return [
        [own, g, d, c, a, e, b, f]
        for own, (a, b, c), (d, e, f), g in zip(panels, near, mid, far)
    ]


def shards(spectra, panels, filters, offsets):
    x, z, yl = lax.axis_index("x"), lax.axis_index("z"), lax.axis_index("yl")
    other_first = panels[1] == LAST
    other = jnp.where(other_first, panels[0], panels[1])
    ox, oz, oy = place_of(other)
    lx, lz, ly = place_of(LAST)
    strip = swap(strips(spectra, other), other, "c")
    arrived = scatter(spectra.reshape(2 * FREQ, ROWS, COLS))
    arrived, strip = lax.optimization_barrier((arrived, strip))
    spot = (oy * 4 + ((ox + 2 * oy) & 3)).astype(jnp.uint32)
    mine = lax.dynamic_index_in_dim(arrived, spot, 0, keepdims=False)
    last = arrived[ly * 4 + (lx + 2 * ly) % 4]
    branches = [lambda v, r=r: leap(v, r) for r in range(8)]
    leapt = lax.switch(oz, branches, mine)
    leapt, last = lax.optimization_barrier((leapt, last))
    mine = land(mine, leapt, oz, z)
    last = land(last, leap(last, lz), lz, z)
    mine, strip = lax.optimization_barrier((mine, strip))
    strip = swap(strip, other, "yh").reshape(2, FREQ, ROWS, 2 * ROWS)
    mine, last = exchange([steps(mine, oz, z, False), steps(last, lz, z, True)])
    blocks = [v for pair in zip(mine, last) for v in pair]
    bins = (x + 2 * yl + jnp.array([0, 2, 3, 1], jnp.int32)) & 3
    left, coefs = tables(filters, offsets, strip, bins, yl)
    return synthesise(bins, spectra, left, coefs, blocks)


def solution(mesh):
    fine = Mesh(mesh.devices.reshape(4, 8, 2, 2, 2), ("x", "z", "yl", "yh", "c"))
    src, rcv = ("x", "z", "yl"), ("yh", "c")
    return jax.shard_map(
        shards,
        mesh=fine,
        in_specs=(P(None, None, src, rcv), P(), P(src, None), P(src)),
        out_specs=P(None, src, rcv),
        check_vma=False,
    )
```

```python
import math

import jax
import jax.numpy as jnp
import numpy as np
from jax import lax
from jax.experimental import pallas as pl
from jax.experimental.pallas import tpu as pltpu
from jax.sharding import Mesh
from jax.sharding import PartitionSpec as P

TWIN = 8
NT = 2048
FIRST_BIN = 64
FREQ = 4
ROWS = 64
COLS = 1024
GROUP = 16
LAST = 63
HI = lax.Precision.HIGHEST


def place_of(panel):
    return panel >> 4, (panel >> 1) & 7, panel & 1


def leap(v, root):
    up = lax.ppermute(v, "z", [(root, (root + 3) % 8)])
    down = lax.ppermute(v, "z", [(root, (root - 3) % 8)])
    return up, down


def land(v, leapt, root, z):
    d = (z - root) & 7
    return jnp.where(d == 0, v, jnp.where(d == 3, leapt[0], leapt[1]))


def steps(held, root, z, exact):
    def pairs(step, away):
        senders = [(root + k) % 8 for k in away] if exact else range(8)
        return [(k, (k + step) % 8) for k in senders]

    after = lax.ppermute(held, "z", pairs(1, (0, 3, 5)))
    before = lax.ppermute(held, "z", pairs(-1, (0, 3)))
    d = (z - root) & 7
    from_after = (d == 1) | (d == 4) | (d == 6)
    from_before = (d == 2) | (d == 7)
    return jnp.where(from_after, after, jnp.where(from_before, before, held))


def strips(spectra, panel):
    flat = spectra.reshape(2 * FREQ, ROWS, COLS)
    start = (panel.astype(jnp.uint32) & 15) * ROWS
    block = jnp.concatenate(
        [lax.dynamic_slice_in_dim(flat, start, ROWS, 2), flat[:, :, COLS - ROWS :]], axis=2
    )
    return block


def opposite(block, axis):
    return lax.ppermute(block, axis, [(0, 1), (1, 0)])


def owned(block, other, panel, axis):
    is_first = lax.broadcasted_iota(jnp.int32, (1, 1, 2 * ROWS), 2) < ROWS
    bit = panel >> 4 & 1 if axis == "c" else panel >> 5
    keep = jnp.where(is_first, bit, 1) == lax.axis_index(axis)
    return jnp.where(keep, block, other)


def partial(sets, bins, x_ref, l_ref, coef_ref, block_refs, before_ref, d_ref, store):
    for n, i in enumerate(sets):
        b = jnp.concatenate([r[...] for r in block_refs[4 * n : 4 * n + 4]], axis=0)
        high = b.astype(jnp.bfloat16)
        low = (b - high.astype(jnp.float32)).astype(jnp.bfloat16)
        f = bins[i]
        left = l_ref[f]
        left_high = left.astype(jnp.bfloat16)
        left_low = (left - left_high.astype(jnp.float32)).astype(jnp.bfloat16)
        both = jnp.dot(
            jnp.concatenate([left_high, left_low], axis=0),
            high,
            preferred_element_type=jnp.float32,
        )
        rest = jnp.dot(left_high, low, preferred_element_type=jnp.float32)
        product = both[: 2 * ROWS] + (both[2 * ROWS :] + rest)
        d_ref[2 * n] = x_ref[0, f] - product[:ROWS]
        d_ref[2 * n + 1] = x_ref[1, f] - product[ROWS:]
    for first in range(0, ROWS, GROUP):
        rows = slice(first, first + GROUP)
        spectrum = [d_ref[k, rows, :] for k in range(2 * len(sets))]
        for u in range(TWIN):
            total = None if before_ref is None else before_ref[u, rows, :]
            for k, value in enumerate(spectrum):
                at = u * 8 + 2 * sets[0] + k
                term = value * coef_ref[rows, at : at + 1]
                total = term if total is None else total + term
            store(u, rows, total)


def early_kernel(bins, x_ref, l_ref, coef_ref, *refs):
    block_refs, o_ref, d_ref = refs[:12], refs[12], refs[13]

    def store(u, rows, total):
        o_ref[u, rows, :] = total

    partial((1, 2, 3), bins, x_ref, l_ref, coef_ref, block_refs, None, d_ref, store)


def late_kernel(bins, x_ref, l_ref, coef_ref, *refs):
    block_refs, before_ref, o_ref, d_ref = refs[:4], refs[4], refs[5], refs[6]

    def store(u, rows, total):
        o_ref[u, rows, :] = total.astype(o_ref.dtype)

    partial((0,), bins, x_ref, l_ref, coef_ref, block_refs, before_ref, d_ref, store)


def synthesise(bins, spectra, left, coefs, blocks):
    vmem = pl.BlockSpec(memory_space=pltpu.VMEM)

    def call(body, sets, dtype, operands):
        return pl.pallas_call(
            body,
            in_specs=[pl.BlockSpec(memory_space=pltpu.SMEM), *[vmem] * len(operands)],
            out_specs=vmem,
            out_shape=jax.ShapeDtypeStruct((TWIN, ROWS, COLS), dtype),
            scratch_shapes=[pltpu.VMEM((2 * sets, ROWS, COLS), jnp.float32)],
            compiler_params=pltpu.CompilerParams(vmem_limit_bytes=24 * 1024 * 1024),
            cost_estimate=pl.CostEstimate(
                flops=2 * 3 * sets * 128 * 256 * COLS,
                bytes_accessed=2 * 2**20 * sets,
                transcendentals=0,
            ),
        )(bins, *operands)

    early = call(early_kernel, 3, jnp.float32, [spectra, left, coefs, *blocks[4:]])
    return call(
        late_kernel, 1, jnp.bfloat16, [spectra, left, coefs, *blocks[:4], early]
    )


def tables(filters, offsets, strip, bins, yl):
    lag = np.arange(64, dtype=np.int64)[:, None] * (FIRST_BIN + np.arange(FREQ))[None, :] % NT
    lag_angle = lag * (2.0 * math.pi / NT)
    response_cos = jnp.dot(filters, jnp.asarray(np.cos(lag_angle), jnp.float32), precision=HI)
    response_sin = jnp.dot(filters, jnp.asarray(np.sin(lag_angle), jnp.float32), precision=HI)
    a_real, a_imag = strip[0], strip[1]
    rc, rs = response_cos.T[:, :, None], response_sin.T[:, :, None]
    real = a_real * rc + a_imag * rs
    imag = a_imag * rc - a_real * rs
    re_first = jnp.concatenate([real, -imag], axis=2)
    im_first = jnp.concatenate([imag, real], axis=2)
    re_last = jnp.concatenate([-imag, real], axis=2)
    im_last = jnp.concatenate([real, imag], axis=2)
    left = jnp.where(
        yl == 0,
        jnp.concatenate([re_first, im_first], axis=1),
        jnp.concatenate([re_last, im_last], axis=1),
    )
    times = offsets[:, None] + jnp.arange(TWIN, dtype=jnp.int32)[None, :]
    phase = times[:, :, None] * (FIRST_BIN + bins)[None, None, :] & (NT - 1)
    angle = phase.astype(jnp.float32) * (2.0 * math.pi / NT)
    coefs = jnp.stack([jnp.cos(angle), -jnp.sin(angle)], axis=3).reshape(ROWS, 64)
    return left, coefs


def scatter(rows):
    members = [(f - 2 * c) % 4 * 2 + c for c in range(2) for f in range(4)]
    return lax.all_to_all(rows, ("x", "yl"), 0, 0, axis_index_groups=[members], tiled=True)


def exchange(panels):
    def send(v, way):
        axis, pairs = {
            "on": ("x", [(i, (i + 1) % 4) for i in range(4)]),
            "back": ("x", [(i, (i - 1) % 4) for i in range(4)]),
            "y": ("yl", [(0, 1), (1, 0)]),
        }[way]
        return lax.ppermute(v, axis, pairs)

    near = [(send(own, "on"), send(own, "back"), send(own, "y")) for own in panels]
    mid = [(send(a, "on"), send(c, "back"), send(a, "y")) for a, _, c in near]
    far = [
        send(d, "y") if i == 0 else send(e, "back") for i, (d, e, _) in enumerate(mid)
    ]
    return [
        [own, g, d, c, a, e, b, f]
        for own, (a, b, c), (d, e, f), g in zip(panels, near, mid, far)
    ]


def shards(spectra, panels, filters, offsets):
    x, z, yl = lax.axis_index("x"), lax.axis_index("z"), lax.axis_index("yl")
    other_first = panels[1] == LAST
    other = jnp.where(other_first, panels[0], panels[1])
    ox, oz, oy = place_of(other)
    lx, lz, ly = place_of(LAST)
    strip = strips(spectra, other)
    strip = owned(strip, opposite(strip, "c"), other, "c")
    arrived = scatter(spectra.reshape(2 * FREQ, ROWS, COLS))
    arrived, strip = lax.optimization_barrier((arrived, strip))
    spot = (oy * 4 + ((ox + 2 * oy) & 3)).astype(jnp.uint32)
    mine = lax.dynamic_index_in_dim(arrived, spot, 0, keepdims=False)
    branches = [lambda v, s, r=r: (leap(v, r), opposite(s, "yh")) for r in range(8)]
    leapt, across = lax.switch(oz, branches, mine, strip)
    leapt, across, arrived = lax.optimization_barrier((leapt, across, arrived))
    mine = land(mine, leapt, oz, z)
    last = arrived[ly * 4 + (lx + 2 * ly) % 4]
    last = land(last, leap(last, lz), lz, z)
    strip = owned(strip, across, other, "yh").reshape(2, FREQ, ROWS, 2 * ROWS)
    mine, last = exchange([steps(mine, oz, z, False), steps(last, lz, z, True)])
    blocks = [v for pair in zip(mine, last) for v in pair]
    bins = (x + 2 * yl + jnp.array([0, 2, 3, 1], jnp.int32)) & 3
    left, coefs = tables(filters, offsets, strip, bins, yl)
    return synthesise(bins, spectra, left, coefs, blocks)


def solution(mesh):
    fine = Mesh(mesh.devices.reshape(4, 8, 2, 2, 2), ("x", "z", "yl", "yh", "c"))
    src, rcv = ("x", "z", "yl"), ("yh", "c")
    return jax.shard_map(
        shards,
        mesh=fine,
        in_specs=(P(None, None, src, rcv), P(), P(src, None), P(src)),
        out_specs=P(None, src, rcv),
        check_vma=False,
    )
```

```python
import math

import jax
import jax.numpy as jnp
import numpy as np
from jax import lax
from jax.experimental import pallas as pl
from jax.experimental.pallas import tpu as pltpu
from jax.sharding import Mesh
from jax.sharding import PartitionSpec as P

TWIN = 8
NT = 2048
FIRST_BIN = 64
FREQ = 4
ROWS = 64
COLS = 1024
GROUP = 16
LAST = 63
HI = lax.Precision.HIGHEST


def place_of(panel):
    return panel >> 4, (panel >> 1) & 7, panel & 1


def leap(v, root):
    up = lax.ppermute(v, "z", [(root, (root + 3) % 8)])
    down = lax.ppermute(v, "z", [(root, (root - 3) % 8)])
    return up, down


def land(v, leapt, root, z):
    d = (z - root) & 7
    return jnp.where(d == 0, v, jnp.where(d == 3, leapt[0], leapt[1]))


def steps(held, root, z, exact):
    def pairs(step, away):
        senders = [(root + k) % 8 for k in away] if exact else range(8)
        return [(k, (k + step) % 8) for k in senders]

    after = lax.ppermute(held, "z", pairs(1, (0, 3, 5)))
    before = lax.ppermute(held, "z", pairs(-1, (0, 3)))
    d = (z - root) & 7
    from_after = (d == 1) | (d == 4) | (d == 6)
    from_before = (d == 2) | (d == 7)
    return jnp.where(from_after, after, jnp.where(from_before, before, held))


def strips(spectra, panel):
    flat = spectra.reshape(2 * FREQ, ROWS, COLS)
    start = (panel.astype(jnp.uint32) & 15) * ROWS
    block = jnp.concatenate(
        [lax.dynamic_slice_in_dim(flat, start, ROWS, 2), flat[:, :, COLS - ROWS :]], axis=2
    )
    return block


def opposite(block, axis):
    return lax.ppermute(block, axis, [(0, 1), (1, 0)])


def owned(block, other, panel, axis):
    is_first = lax.broadcasted_iota(jnp.int32, (1, 1, 2 * ROWS), 2) < ROWS
    bit = panel >> 4 & 1 if axis == "c" else panel >> 5
    keep = jnp.where(is_first, bit, 1) == lax.axis_index(axis)
    return jnp.where(keep, block, other)


def partial(sets, bins, x_ref, l_ref, coef_ref, block_refs, before_ref, d_ref, store):
    for n, i in enumerate(sets):
        b = jnp.concatenate([r[...] for r in block_refs[4 * n : 4 * n + 4]], axis=0)
        high = b.astype(jnp.bfloat16)
        low = (b - high.astype(jnp.float32)).astype(jnp.bfloat16)
        f = bins[i]
        left = l_ref[f]
        left_high = left.astype(jnp.bfloat16)
        left_low = (left - left_high.astype(jnp.float32)).astype(jnp.bfloat16)
        both = jnp.dot(
            jnp.concatenate([left_high, left_low], axis=0),
            high,
            preferred_element_type=jnp.float32,
        )
        rest = jnp.dot(left_high, low, preferred_element_type=jnp.float32)
        product = both[: 2 * ROWS] + (both[2 * ROWS :] + rest)
        d_ref[2 * n] = x_ref[0, f] - product[:ROWS]
        d_ref[2 * n + 1] = x_ref[1, f] - product[ROWS:]
    for first in range(0, ROWS, GROUP):
        rows = slice(first, first + GROUP)
        spectrum = [d_ref[k, rows, :] for k in range(2 * len(sets))]
        for u in range(TWIN):
            total = None if before_ref is None else before_ref[u, rows, :]
            for k, value in enumerate(spectrum):
                at = u * 8 + 2 * sets[0] + k
                term = value * coef_ref[rows, at : at + 1]
                total = term if total is None else total + term
            store(u, rows, total)


def early_kernel(bins, x_ref, l_ref, coef_ref, *refs):
    block_refs, o_ref, d_ref = refs[:12], refs[12], refs[13]

    def store(u, rows, total):
        o_ref[u, rows, :] = total

    partial((1, 2, 3), bins, x_ref, l_ref, coef_ref, block_refs, None, d_ref, store)


def late_kernel(bins, x_ref, l_ref, coef_ref, *refs):
    block_refs, before_ref, o_ref, d_ref = refs[:4], refs[4], refs[5], refs[6]

    def store(u, rows, total):
        o_ref[u, rows, :] = total.astype(o_ref.dtype)

    partial((0,), bins, x_ref, l_ref, coef_ref, block_refs, before_ref, d_ref, store)


def synthesise(bins, spectra, left, coefs, blocks):
    vmem = pl.BlockSpec(memory_space=pltpu.VMEM)

    def call(body, sets, dtype, operands):
        return pl.pallas_call(
            body,
            in_specs=[pl.BlockSpec(memory_space=pltpu.SMEM), *[vmem] * len(operands)],
            out_specs=vmem,
            out_shape=jax.ShapeDtypeStruct((TWIN, ROWS, COLS), dtype),
            scratch_shapes=[pltpu.VMEM((2 * sets, ROWS, COLS), jnp.float32)],
            compiler_params=pltpu.CompilerParams(vmem_limit_bytes=24 * 1024 * 1024),
            cost_estimate=pl.CostEstimate(
                flops=2 * 3 * sets * 128 * 256 * COLS,
                bytes_accessed=2 * 2**20 * sets,
                transcendentals=0,
            ),
        )(bins, *operands)

    early = call(early_kernel, 3, jnp.float32, [spectra, left, coefs, *blocks[4:]])
    return call(
        late_kernel, 1, jnp.bfloat16, [spectra, left, coefs, *blocks[:4], early]
    )


def tables(filters, offsets, strip, bins, yl):
    lag = np.arange(64, dtype=np.int64)[:, None] * (FIRST_BIN + np.arange(FREQ))[None, :] % NT
    lag_angle = lag * (2.0 * math.pi / NT)
    response_cos = jnp.dot(filters, jnp.asarray(np.cos(lag_angle), jnp.float32), precision=HI)
    response_sin = jnp.dot(filters, jnp.asarray(np.sin(lag_angle), jnp.float32), precision=HI)
    a_real, a_imag = strip[0], strip[1]
    rc, rs = response_cos.T[:, :, None], response_sin.T[:, :, None]
    real = a_real * rc + a_imag * rs
    imag = a_imag * rc - a_real * rs
    re_first = jnp.concatenate([real, -imag], axis=2)
    im_first = jnp.concatenate([imag, real], axis=2)
    re_last = jnp.concatenate([-imag, real], axis=2)
    im_last = jnp.concatenate([real, imag], axis=2)
    left = jnp.where(
        yl == 0,
        jnp.concatenate([re_first, im_first], axis=1),
        jnp.concatenate([re_last, im_last], axis=1),
    )
    times = offsets[:, None] + jnp.arange(TWIN, dtype=jnp.int32)[None, :]
    phase = times[:, :, None] * (FIRST_BIN + bins)[None, None, :] & (NT - 1)
    angle = phase.astype(jnp.float32) * (2.0 * math.pi / NT)
    coefs = jnp.stack([jnp.cos(angle), -jnp.sin(angle)], axis=3).reshape(ROWS, 64)
    return left, coefs


def scatter(rows):
    members = [(f - 2 * c) % 4 * 2 + c for c in range(2) for f in range(4)]
    return lax.all_to_all(rows, ("x", "yl"), 0, 0, axis_index_groups=[members], tiled=True)


def exchange(panels):
    def send(v, way):
        axis, pairs = {
            "on": ("x", [(i, (i + 1) % 4) for i in range(4)]),
            "back": ("x", [(i, (i - 1) % 4) for i in range(4)]),
            "y": ("yl", [(0, 1), (1, 0)]),
        }[way]
        return lax.ppermute(v, axis, pairs)

    near = [(send(own, "on"), send(own, "back"), send(own, "y")) for own in panels]
    mid = [(send(a, "on"), send(c, "back"), send(a, "y")) for a, _, c in near]
    far = [
        send(d, "y") if i == 0 else send(e, "back") for i, (d, e, _) in enumerate(mid)
    ]
    return [
        [own, g, d, c, a, e, b, f]
        for own, (a, b, c), (d, e, f), g in zip(panels, near, mid, far)
    ]


def shards(spectra, panels, filters, offsets):
    x, z, yl = lax.axis_index("x"), lax.axis_index("z"), lax.axis_index("yl")
    other_first = panels[1] == LAST
    other = jnp.where(other_first, panels[0], panels[1])
    ox, oz, oy = place_of(other)
    lx, lz, ly = place_of(LAST)
    strip = strips(spectra, other)
    strip = owned(strip, opposite(strip, "c"), other, "c")
    arrived = scatter(spectra.reshape(2 * FREQ, ROWS, COLS))
    arrived, strip = lax.optimization_barrier((arrived, strip))
    spot = (oy * 4 + ((ox + 2 * oy) & 3)).astype(jnp.uint32)
    mine = lax.dynamic_index_in_dim(arrived, spot, 0, keepdims=False)
    last = arrived[ly * 4 + (lx + 2 * ly) % 4]

    def branch(root):
        return lambda a, b, block: (leap(a, root), leap(b, lz), opposite(block, "yh"))

    leapt, last_leapt, across = lax.switch(
        oz, [branch(r) for r in range(8)], mine, last, strip
    )
    mine, last = land(mine, leapt, oz, z), land(last, last_leapt, lz, z)
    strip = owned(strip, across, other, "yh").reshape(2, FREQ, ROWS, 2 * ROWS)
    mine, last = exchange([steps(mine, oz, z, False), steps(last, lz, z, True)])
    blocks = [v for pair in zip(mine, last) for v in pair]
    bins = (x + 2 * yl + jnp.array([0, 2, 3, 1], jnp.int32)) & 3
    left, coefs = tables(filters, offsets, strip, bins, yl)
    return synthesise(bins, spectra, left, coefs, blocks)


def solution(mesh):
    fine = Mesh(mesh.devices.reshape(4, 8, 2, 2, 2), ("x", "z", "yl", "yh", "c"))
    src, rcv = ("x", "z", "yl"), ("yh", "c")
    return jax.shard_map(
        shards,
        mesh=fine,
        in_specs=(P(None, None, src, rcv), P(), P(src, None), P(src)),
        out_specs=P(None, src, rcv),
        check_vma=False,
    )
```

```python
import math

import jax
import jax.numpy as jnp
import numpy as np
from jax import lax
from jax.experimental import pallas as pl
from jax.experimental.pallas import tpu as pltpu
from jax.sharding import Mesh
from jax.sharding import PartitionSpec as P

TWIN = 8
NT = 2048
FIRST_BIN = 64
FREQ = 4
ROWS = 64
COLS = 1024
GROUP = 16
LAST = 63
HI = lax.Precision.HIGHEST


def place_of(panel):
    return panel >> 4, (panel >> 1) & 7, panel & 1


def leap(v, root):
    up = lax.ppermute(v, "z", [(root, (root + 3) % 8)])
    down = lax.ppermute(v, "z", [(root, (root - 3) % 8)])
    return up, down


def land(v, leapt, root, z):
    d = (z - root) & 7
    return jnp.where(d == 0, v, jnp.where(d == 3, leapt[0], leapt[1]))


def steps(held, root, z, exact):
    def pairs(step, away):
        senders = [(root + k) % 8 for k in away] if exact else range(8)
        return [(k, (k + step) % 8) for k in senders]

    after = lax.ppermute(held, "z", pairs(1, (0, 3, 5)))
    before = lax.ppermute(held, "z", pairs(-1, (0, 3)))
    d = (z - root) & 7
    from_after = (d == 1) | (d == 4) | (d == 6)
    from_before = (d == 2) | (d == 7)
    return jnp.where(from_after, after, jnp.where(from_before, before, held))


def strips(spectra, panel):
    flat = spectra.reshape(2 * FREQ, ROWS, COLS)
    start = (panel.astype(jnp.uint32) & 15) * ROWS
    block = jnp.concatenate(
        [lax.dynamic_slice_in_dim(flat, start, ROWS, 2), flat[:, :, COLS - ROWS :]], axis=2
    )
    return block


def opposite(block, axis):
    return lax.ppermute(block, axis, [(0, 1), (1, 0)])


def owned(block, other, panel, axis):
    is_first = lax.broadcasted_iota(jnp.int32, (1, 1, 2 * ROWS), 2) < ROWS
    bit = panel >> 4 & 1 if axis == "c" else panel >> 5
    keep = jnp.where(is_first, bit, 1) == lax.axis_index(axis)
    return jnp.where(keep, block, other)


def product(left, part, block_refs):
    left = left[:, part * 2 * ROWS : (part + 1) * 2 * ROWS]
    b = jnp.concatenate([r[...] for r in block_refs], axis=0)
    high = b.astype(jnp.bfloat16)
    low = (b - high.astype(jnp.float32)).astype(jnp.bfloat16)
    left_high = left.astype(jnp.bfloat16)
    left_low = (left - left_high.astype(jnp.float32)).astype(jnp.bfloat16)
    both = jnp.dot(
        jnp.concatenate([left_high, left_low], axis=0),
        high,
        preferred_element_type=jnp.float32,
    )
    rest = jnp.dot(left_high, low, preferred_element_type=jnp.float32)
    return both[: 2 * ROWS] + (both[2 * ROWS :] + rest)


def synthesis(planes_ref, first_plane, count, coef_ref, before_ref, o_ref):
    for first in range(0, ROWS, GROUP):
        rows = slice(first, first + GROUP)
        planes = [planes_ref[k, rows, :] for k in range(count)]
        for u in range(TWIN):
            total = None if before_ref is None else before_ref[u, rows, :]
            for k, value in enumerate(planes):
                at = u * 8 + first_plane + k
                term = value * coef_ref[rows, at : at + 1]
                total = term if total is None else total + term
            o_ref[u, rows, :] = total.astype(o_ref.dtype)


def first_kernel(bins, x_ref, l_ref, *refs):
    block_refs, d_ref = refs[:8], refs[8]
    for i, part in enumerate((0, 1, 0, 0)):
        f = bins[i]
        p = product(l_ref[f], part, block_refs[2 * i : 2 * i + 2])
        d_ref[2 * i] = x_ref[0, f] - p[:ROWS]
        d_ref[2 * i + 1] = x_ref[1, f] - p[ROWS:]


def second_kernel(bins, d_ref, l_ref, coef_ref, *refs):
    block_refs, o_ref, e_ref = refs[:6], refs[6], refs[7]
    for n, part in enumerate((0, 1, 1)):
        p = product(l_ref[bins[n + 1]], part, block_refs[2 * n : 2 * n + 2])
        e_ref[2 * n] = d_ref[2 * n + 2] - p[:ROWS]
        e_ref[2 * n + 1] = d_ref[2 * n + 3] - p[ROWS:]
    synthesis(e_ref, 2, 6, coef_ref, None, o_ref)


def third_kernel(bins, d_ref, l_ref, coef_ref, mine_ref, last_ref, before_ref, o_ref, e_ref):
    p = product(l_ref[bins[0]], 1, (mine_ref, last_ref))
    e_ref[0] = d_ref[0] - p[:ROWS]
    e_ref[1] = d_ref[1] - p[ROWS:]
    synthesis(e_ref, 0, 2, coef_ref, before_ref, o_ref)


def synthesise(bins, spectra, left, coefs, mine, last):
    vmem = pl.BlockSpec(memory_space=pltpu.VMEM)

    def call(body, halves, dtype, scratch, operands):
        return pl.pallas_call(
            body,
            in_specs=[pl.BlockSpec(memory_space=pltpu.SMEM), *[vmem] * len(operands)],
            out_specs=vmem,
            out_shape=jax.ShapeDtypeStruct((TWIN, ROWS, COLS), dtype),
            scratch_shapes=[pltpu.VMEM((n, ROWS, COLS), jnp.float32) for n in scratch],
            compiler_params=pltpu.CompilerParams(vmem_limit_bytes=24 * 1024 * 1024),
            cost_estimate=pl.CostEstimate(
                flops=2 * 3 * halves * 128 * 128 * COLS,
                bytes_accessed=2**20 * halves,
                transcendentals=0,
            ),
        )(bins, *operands)

    def pick(*places):
        return [v[k] for k in places for v in (mine, last)]

    planes = call(first_kernel, 4, jnp.float32, [], [spectra, left, *pick(0, 3, 4, 6)])
    totals = call(
        second_kernel, 3, jnp.float32, [6], [planes, left, coefs, *pick(2, 5, 7)]
    )
    return call(
        third_kernel, 1, jnp.bfloat16, [2], [planes, left, coefs, *pick(1), totals]
    )


def tables(filters, offsets, strip, bins, yl):
    lag = np.arange(64, dtype=np.int64)[:, None] * (FIRST_BIN + np.arange(FREQ))[None, :] % NT
    lag_angle = lag * (2.0 * math.pi / NT)
    response_cos = jnp.dot(filters, jnp.asarray(np.cos(lag_angle), jnp.float32), precision=HI)
    response_sin = jnp.dot(filters, jnp.asarray(np.sin(lag_angle), jnp.float32), precision=HI)
    a_real, a_imag = strip[0], strip[1]
    rc, rs = response_cos.T[:, :, None], response_sin.T[:, :, None]
    real = a_real * rc + a_imag * rs
    imag = a_imag * rc - a_real * rs
    re_first = jnp.concatenate([real, -imag], axis=2)
    im_first = jnp.concatenate([imag, real], axis=2)
    re_last = jnp.concatenate([-imag, real], axis=2)
    im_last = jnp.concatenate([real, imag], axis=2)
    left = jnp.where(
        yl == 0,
        jnp.concatenate([re_first, im_first], axis=1),
        jnp.concatenate([re_last, im_last], axis=1),
    )
    times = offsets[:, None] + jnp.arange(TWIN, dtype=jnp.int32)[None, :]
    phase = times[:, :, None] * (FIRST_BIN + bins)[None, None, :] & (NT - 1)
    angle = phase.astype(jnp.float32) * (2.0 * math.pi / NT)
    coefs = jnp.stack([jnp.cos(angle), -jnp.sin(angle)], axis=3).reshape(ROWS, 64)
    return left, coefs


def scatter(rows):
    members = [(f - 2 * c) % 4 * 2 + c for c in range(2) for f in range(4)]
    return lax.all_to_all(rows, ("x", "yl"), 0, 0, axis_index_groups=[members], tiled=True)


def exchange(panels):
    def send(v, way):
        axis, pairs = {
            "on": ("x", [(i, (i + 1) % 4) for i in range(4)]),
            "back": ("x", [(i, (i - 1) % 4) for i in range(4)]),
            "y": ("yl", [(0, 1), (1, 0)]),
        }[way]
        return lax.ppermute(v, axis, pairs)

    near = [(send(own, "on"), send(own, "back"), send(own, "y")) for own in panels]
    mid = [(send(a, "on"), send(c, "back"), send(a, "y")) for a, _, c in near]
    far = [
        send(d, "y") if i == 0 else send(e, "back") for i, (d, e, _) in enumerate(mid)
    ]
    return [
        [own, g, d, c, a, e, b, f]
        for own, (a, b, c), (d, e, f), g in zip(panels, near, mid, far)
    ]


def shards(spectra, panels, filters, offsets):
    x, z, yl = lax.axis_index("x"), lax.axis_index("z"), lax.axis_index("yl")
    other_first = panels[1] == LAST
    other = jnp.where(other_first, panels[0], panels[1])
    ox, oz, oy = place_of(other)
    lx, lz, ly = place_of(LAST)
    strip = strips(spectra, other)
    strip = owned(strip, opposite(strip, "c"), other, "c")
    arrived = scatter(spectra.reshape(2 * FREQ, ROWS, COLS))
    arrived, strip = lax.optimization_barrier((arrived, strip))
    spot = (oy * 4 + ((ox + 2 * oy) & 3)).astype(jnp.uint32)
    mine = lax.dynamic_index_in_dim(arrived, spot, 0, keepdims=False)
    last = arrived[ly * 4 + (lx + 2 * ly) % 4]

    def branch(root):
        return lambda a, b, block: (leap(a, root), leap(b, lz), opposite(block, "yh"))

    leapt, last_leapt, across = lax.switch(
        oz, [branch(r) for r in range(8)], mine, last, strip
    )
    mine, last = land(mine, leapt, oz, z), land(last, last_leapt, lz, z)
    strip = owned(strip, across, other, "yh").reshape(2, FREQ, ROWS, 2 * ROWS)
    mine, last = exchange([steps(mine, oz, z, False), steps(last, lz, z, True)])
    bins = (x + 2 * yl + jnp.array([0, 2, 3, 1], jnp.int32)) & 3
    left, coefs = tables(filters, offsets, strip, bins, yl)
    return synthesise(bins, spectra, left, coefs, mine, last)


def solution(mesh):
    fine = Mesh(mesh.devices.reshape(4, 8, 2, 2, 2), ("x", "z", "yl", "yh", "c"))
    src, rcv = ("x", "z", "yl"), ("yh", "c")
    return jax.shard_map(
        shards,
        mesh=fine,
        in_specs=(P(None, None, src, rcv), P(), P(src, None), P(src)),
        out_specs=P(None, src, rcv),
        check_vma=False,
    )
```

```python
import math

import jax
import jax.numpy as jnp
import numpy as np
from jax import lax
from jax.experimental import pallas as pl
from jax.experimental.pallas import tpu as pltpu
from jax.sharding import Mesh
from jax.sharding import PartitionSpec as P

TWIN = 8
NT = 2048
FIRST_BIN = 64
FREQ = 4
ROWS = 64
COLS = 1024
GROUP = 16
LAST = 63
HI = lax.Precision.HIGHEST


def place_of(panel):
    return panel >> 4, (panel >> 1) & 7, panel & 1


def leap(v, root):
    up = lax.ppermute(v, "z", [(root, (root + 3) % 8)])
    down = lax.ppermute(v, "z", [(root, (root - 3) % 8)])
    return up, down


def choose(cases, n, *arrays):
    def body(cases_ref, *refs):
        for k, ref in enumerate(refs[:-1]):

            @pl.when(cases_ref[n] == k)
            def _():
                refs[-1][...] = ref[...]

    vmem = pl.BlockSpec(memory_space=pltpu.VMEM)
    return pl.pallas_call(
        body,
        in_specs=[pl.BlockSpec(memory_space=pltpu.SMEM), *[vmem] * len(arrays)],
        out_specs=vmem,
        out_shape=jax.ShapeDtypeStruct(arrays[0].shape, arrays[0].dtype),
        cost_estimate=pl.CostEstimate(flops=0, bytes_accessed=2**19, transcendentals=0),
    )(cases, *arrays)


def land_case(root, z):
    d = (z - root) & 7
    return jnp.where(d == 0, 0, jnp.where(d == 3, 1, 2))


def steps(held, root, z, exact):
    def pairs(step, away):
        senders = [(root + k) % 8 for k in away] if exact else range(8)
        return [(k, (k + step) % 8) for k in senders]

    below = lax.ppermute(held, "z", pairs(1, (0, 3, 5)))
    above = lax.ppermute(held, "z", pairs(-1, (0, 3)))
    d = (z - root) & 7
    from_below = (d == 1) | (d == 4) | (d == 6)
    from_above = (d == 2) | (d == 7)
    return jnp.where(from_below, below, jnp.where(from_above, above, held))


def strips(spectra, panel):
    flat = spectra.reshape(2 * FREQ, ROWS, COLS)
    start = (panel.astype(jnp.uint32) & 15) * ROWS
    block = jnp.concatenate(
        [lax.dynamic_slice_in_dim(flat, start, ROWS, 2), flat[:, :, COLS - ROWS :]], axis=2
    )
    return block


def opposite(block, axis):
    return lax.ppermute(block, axis, [(0, 1), (1, 0)])


def owned(block, other, panel, axis):
    is_first = lax.broadcasted_iota(jnp.int32, (1, 1, 2 * ROWS), 2) < ROWS
    bit = panel >> 4 & 1 if axis == "c" else panel >> 5
    keep = jnp.where(is_first, bit, 1) == lax.axis_index(axis)
    return jnp.where(keep, block, other)


def product(left, part, block_refs):
    left = left[:, part * 2 * ROWS : (part + 1) * 2 * ROWS]
    b = jnp.concatenate([r[...] for r in block_refs], axis=0)
    high = b.astype(jnp.bfloat16)
    low = (b - high.astype(jnp.float32)).astype(jnp.bfloat16)
    left_high = left.astype(jnp.bfloat16)
    left_low = (left - left_high.astype(jnp.float32)).astype(jnp.bfloat16)
    both = jnp.dot(
        jnp.concatenate([left_high, left_low], axis=0),
        high,
        preferred_element_type=jnp.float32,
    )
    rest = jnp.dot(left_high, low, preferred_element_type=jnp.float32)
    return both[: 2 * ROWS] + (both[2 * ROWS :] + rest)


def synthesis(planes_ref, first_plane, count, coef_ref, before_ref, o_ref, done=None):
    for first in range(0, ROWS, GROUP):
        rows = slice(first, first + GROUP)
        planes = [planes_ref[k, rows, :] for k in range(count)]
        for u in range(TWIN):
            total = None if before_ref is None else before_ref[u, rows, :]
            for k, value in enumerate(planes):
                at = u * 8 + first_plane + k
                term = value * coef_ref[rows, at : at + 1]
                total = term if total is None else total + term
            o_ref[u, rows, :] = total.astype(o_ref.dtype)
        if done is not None:
            done(first // GROUP)


def first_kernel(bins, x_ref, l_ref, *refs):
    block_refs, d_ref = refs[:8], refs[8]
    for i, part in enumerate((0, 1, 0, 0)):
        f = bins[i]
        p = product(l_ref[f], part, block_refs[2 * i : 2 * i + 2])
        d_ref[2 * i] = x_ref[0, f] - p[:ROWS]
        d_ref[2 * i + 1] = x_ref[1, f] - p[ROWS:]


def second_kernel(bins, d_ref, l_ref, coef_ref, *refs):
    block_refs, o_ref, e_ref = refs[:6], refs[6], refs[7]
    for n, part in enumerate((0, 1, 1)):
        p = product(l_ref[bins[n + 1]], part, block_refs[2 * n : 2 * n + 2])
        e_ref[2 * n] = d_ref[2 * n + 2] - p[:ROWS]
        e_ref[2 * n + 1] = d_ref[2 * n + 3] - p[ROWS:]
    synthesis(e_ref, 2, 6, coef_ref, None, o_ref)


def third_kernel(
    bins, d_ref, l_ref, coef_ref, mine_ref, last_ref, before_ref, o_ref, e_ref, out_ref, sem
):
    p = product(l_ref[bins[0]], 1, (mine_ref, last_ref))
    e_ref[0] = d_ref[0] - p[:ROWS]
    e_ref[1] = d_ref[1] - p[ROWS:]

    def copy(k):
        rows = pl.ds(k * GROUP, GROUP)
        return pltpu.make_async_copy(out_ref.at[:, rows], o_ref.at[:, rows], sem.at[k])

    synthesis(e_ref, 0, 2, coef_ref, before_ref, out_ref, lambda k: copy(k).start())
    for k in range(ROWS // GROUP):
        copy(k).wait()


def synthesise(bins, spectra, left, coefs, mine, last):
    vmem = pl.BlockSpec(memory_space=pltpu.VMEM)

    def call(body, halves, scratch, operands, out=vmem, dtype=jnp.float32):
        return pl.pallas_call(
            body,
            in_specs=[pl.BlockSpec(memory_space=pltpu.SMEM), *[vmem] * len(operands)],
            out_specs=out,
            out_shape=jax.ShapeDtypeStruct((TWIN, ROWS, COLS), dtype),
            scratch_shapes=scratch,
            compiler_params=pltpu.CompilerParams(vmem_limit_bytes=24 * 1024 * 1024),
            cost_estimate=pl.CostEstimate(
                flops=2 * 3 * halves * 128 * 128 * COLS,
                bytes_accessed=2**20 * halves,
                transcendentals=0,
            ),
        )(bins, *operands)

    def held(n):
        return pltpu.VMEM((n, ROWS, COLS), jnp.float32)

    def pick(*places):
        return [v[k] for k in places for v in (mine, last)]

    planes = call(first_kernel, 4, [], [spectra, left, *pick(0, 3, 4, 6)])
    totals = call(second_kernel, 3, [held(6)], [planes, left, coefs, *pick(2, 5, 7)])
    pieces = [
        held(2),
        pltpu.VMEM((TWIN, ROWS, COLS), jnp.bfloat16),
        pltpu.SemaphoreType.DMA((ROWS // GROUP,)),
    ]
    operands = [planes, left, coefs, *pick(1), totals]
    return call(
        third_kernel, 1, pieces, operands, pl.BlockSpec(memory_space=pl.ANY), jnp.bfloat16
    )


def tables(filters, offsets, strip, bins, yl):
    lag = np.arange(64, dtype=np.int64)[:, None] * (FIRST_BIN + np.arange(FREQ))[None, :] % NT
    lag_angle = lag * (2.0 * math.pi / NT)
    response_cos = jnp.dot(filters, jnp.asarray(np.cos(lag_angle), jnp.float32), precision=HI)
    response_sin = jnp.dot(filters, jnp.asarray(np.sin(lag_angle), jnp.float32), precision=HI)
    a_real, a_imag = strip[0], strip[1]
    rc, rs = response_cos.T[:, :, None], response_sin.T[:, :, None]
    real = a_real * rc + a_imag * rs
    imag = a_imag * rc - a_real * rs
    re_first = jnp.concatenate([real, -imag], axis=2)
    im_first = jnp.concatenate([imag, real], axis=2)
    re_last = jnp.concatenate([-imag, real], axis=2)
    im_last = jnp.concatenate([real, imag], axis=2)
    left = jnp.where(
        yl == 0,
        jnp.concatenate([re_first, im_first], axis=1),
        jnp.concatenate([re_last, im_last], axis=1),
    )
    times = offsets[:, None] + jnp.arange(TWIN, dtype=jnp.int32)[None, :]
    phase = times[:, :, None] * (FIRST_BIN + bins)[None, None, :] & (NT - 1)
    angle = phase.astype(jnp.float32) * (2.0 * math.pi / NT)
    coefs = jnp.stack([jnp.cos(angle), -jnp.sin(angle)], axis=3).reshape(ROWS, 64)
    return left, coefs


def scatter(rows):
    members = [(f - 2 * c) % 4 * 2 + c for c in range(2) for f in range(4)]
    return lax.all_to_all(rows, ("x", "yl"), 0, 0, axis_index_groups=[members], tiled=True)


def exchange(panels):
    def send(v, way):
        axis, pairs = {
            "on": ("x", [(i, (i + 1) % 4) for i in range(4)]),
            "back": ("x", [(i, (i - 1) % 4) for i in range(4)]),
            "y": ("yl", [(0, 1), (1, 0)]),
        }[way]
        return lax.ppermute(v, axis, pairs)

    near = [(send(own, "on"), send(own, "back"), send(own, "y")) for own in panels]
    mid = [(send(a, "on"), send(c, "back"), send(a, "y")) for a, _, c in near]
    far = [
        send(d, "y") if i == 0 else send(e, "back") for i, (d, e, _) in enumerate(mid)
    ]
    return [
        [own, g, d, c, a, e, b, f]
        for own, (a, b, c), (d, e, f), g in zip(panels, near, mid, far)
    ]


def shards(spectra, panels, filters, offsets):
    x, z, yl = lax.axis_index("x"), lax.axis_index("z"), lax.axis_index("yl")
    other_first = panels[1] == LAST
    other = jnp.where(other_first, panels[0], panels[1])
    ox, oz, oy = place_of(other)
    lx, lz, ly = place_of(LAST)
    cases = jnp.stack([land_case(oz, z), land_case(lz, z)])
    strip = strips(spectra, other)
    strip = owned(strip, opposite(strip, "c"), other, "c")
    arrived = scatter(spectra.reshape(2 * FREQ, ROWS, COLS))
    arrived, strip = lax.optimization_barrier((arrived, strip))
    spot = (oy * 4 + ((ox + 2 * oy) & 3)).astype(jnp.uint32)
    mine = lax.dynamic_index_in_dim(arrived, spot, 0, keepdims=False)
    last = arrived[ly * 4 + (lx + 2 * ly) % 4]

    def branch(root):
        return lambda a, b, block: (leap(a, root), leap(b, lz), opposite(block, "yh"))

    leapt, last_leapt, across = lax.switch(
        oz, [branch(r) for r in range(8)], mine, last, strip
    )
    mine, last = choose(cases, 0, mine, *leapt), choose(cases, 1, last, *last_leapt)
    strip = owned(strip, across, other, "yh").reshape(2, FREQ, ROWS, 2 * ROWS)
    mine, last = exchange([steps(mine, oz, z, False), steps(last, lz, z, True)])
    bins = (x + 2 * yl + jnp.array([0, 2, 3, 1], jnp.int32)) & 3
    left, coefs = tables(filters, offsets, strip, bins, yl)
    return synthesise(bins, spectra, left, coefs, mine, last)


def solution(mesh):
    fine = Mesh(mesh.devices.reshape(4, 8, 2, 2, 2), ("x", "z", "yl", "yh", "c"))
    src, rcv = ("x", "z", "yl"), ("yh", "c")
    return jax.shard_map(
        shards,
        mesh=fine,
        in_specs=(P(None, None, src, rcv), P(), P(src, None), P(src)),
        out_specs=P(None, src, rcv),
        check_vma=False,
    )
```

```python
import math

import jax
import jax.numpy as jnp
import numpy as np
from jax import lax
from jax.experimental import pallas as pl
from jax.experimental.pallas import tpu as pltpu
from jax.sharding import Mesh
from jax.sharding import PartitionSpec as P

TWIN = 8
NT = 2048
FIRST_BIN = 64
FREQ = 4
ROWS = 64
COLS = 1024
GROUP = 16
LAST = 63
HI = lax.Precision.HIGHEST


def place_of(panel):
    return panel >> 4, (panel >> 1) & 7, panel & 1


def leap(v, root):
    up = lax.ppermute(v, "z", [(root, (root + 3) % 8)])
    down = lax.ppermute(v, "z", [(root, (root - 3) % 8)])
    return up, down


def land(v, leapt, root, z):
    d = (z - root) & 7
    return jnp.where(d == 0, v, jnp.where(d == 3, leapt[0], leapt[1]))


def steps(held, root, z, exact):
    def pairs(step, away):
        senders = [(root + k) % 8 for k in away] if exact else range(8)
        return [(k, (k + step) % 8) for k in senders]

    below = lax.ppermute(held, "z", pairs(1, (0, 3, 5)))
    above = lax.ppermute(held, "z", pairs(-1, (0, 3)))
    d = (z - root) & 7
    from_below = (d == 1) | (d == 4) | (d == 6)
    from_above = (d == 2) | (d == 7)
    return jnp.where(from_below, below, jnp.where(from_above, above, held))


def strips(spectra, panel):
    flat = spectra.reshape(2 * FREQ, ROWS, COLS)
    start = (panel.astype(jnp.uint32) & 15) * ROWS
    block = jnp.concatenate(
        [lax.dynamic_slice_in_dim(flat, start, ROWS, 2), flat[:, :, COLS - ROWS :]], axis=2
    )
    return block


def opposite(block, axis):
    return lax.ppermute(block, axis, [(0, 1), (1, 0)])


def owned(block, other, panel, axis):
    is_first = lax.broadcasted_iota(jnp.int32, (1, 1, 2 * ROWS), 2) < ROWS
    bit = panel >> 4 & 1 if axis == "c" else panel >> 5
    keep = jnp.where(is_first, bit, 1) == lax.axis_index(axis)
    return jnp.where(keep, block, other)


def product(left, part, block_refs):
    left = left[:, part * 2 * ROWS : (part + 1) * 2 * ROWS]
    b = jnp.concatenate([r[...] for r in block_refs], axis=0)
    high = b.astype(jnp.bfloat16)
    low = (b - high.astype(jnp.float32)).astype(jnp.bfloat16)
    left_high = left.astype(jnp.bfloat16)
    left_low = (left - left_high.astype(jnp.float32)).astype(jnp.bfloat16)
    both = jnp.dot(
        jnp.concatenate([left_high, left_low], axis=0),
        high,
        preferred_element_type=jnp.float32,
    )
    rest = jnp.dot(left_high, low, preferred_element_type=jnp.float32)
    return both[: 2 * ROWS] + (both[2 * ROWS :] + rest)


def synthesis(planes_ref, first_plane, count, coef_ref, before_ref, o_ref, done=None):
    for first in range(0, ROWS, GROUP):
        rows = slice(first, first + GROUP)
        planes = [planes_ref[k, rows, :] for k in range(count)]
        for u in range(TWIN):
            total = None if before_ref is None else before_ref[u, rows, :]
            for k, value in enumerate(planes):
                at = u * 8 + first_plane + k
                term = value * coef_ref[rows, at : at + 1]
                total = term if total is None else total + term
            o_ref[u, rows, :] = total.astype(o_ref.dtype)
        if done is not None:
            done(first // GROUP)


def first_kernel(bins, x_ref, l_ref, *refs):
    block_refs, d_ref = refs[:8], refs[8]
    for i, part in enumerate((0, 1, 0, 0)):
        f = bins[i]
        p = product(l_ref[f], part, block_refs[2 * i : 2 * i + 2])
        d_ref[2 * i] = x_ref[0, f] - p[:ROWS]
        d_ref[2 * i + 1] = x_ref[1, f] - p[ROWS:]


def second_kernel(bins, d_ref, l_ref, coef_ref, *refs):
    block_refs, o_ref, e_ref = refs[:6], refs[6], refs[7]
    for n, part in enumerate((0, 1, 1)):
        p = product(l_ref[bins[n + 1]], part, block_refs[2 * n : 2 * n + 2])
        e_ref[2 * n] = d_ref[2 * n + 2] - p[:ROWS]
        e_ref[2 * n + 1] = d_ref[2 * n + 3] - p[ROWS:]
    synthesis(e_ref, 2, 6, coef_ref, None, o_ref)


def third_kernel(
    bins, d_ref, l_ref, coef_ref, mine_ref, last_ref, before_ref, o_ref, e_ref, out_ref, sem
):
    p = product(l_ref[bins[0]], 1, (mine_ref, last_ref))
    e_ref[0] = d_ref[0] - p[:ROWS]
    e_ref[1] = d_ref[1] - p[ROWS:]

    def copy(k):
        rows = pl.ds(k * GROUP, GROUP)
        return pltpu.make_async_copy(out_ref.at[:, rows], o_ref.at[:, rows], sem.at[k])

    synthesis(e_ref, 0, 2, coef_ref, before_ref, out_ref, lambda k: copy(k).start())
    for k in range(ROWS // GROUP):
        copy(k).wait()


def synthesise(bins, spectra, left, coefs, mine, last):
    vmem = pl.BlockSpec(memory_space=pltpu.VMEM)

    def call(body, halves, scratch, operands, out=vmem, dtype=jnp.float32):
        return pl.pallas_call(
            body,
            in_specs=[pl.BlockSpec(memory_space=pltpu.SMEM), *[vmem] * len(operands)],
            out_specs=out,
            out_shape=jax.ShapeDtypeStruct((TWIN, ROWS, COLS), dtype),
            scratch_shapes=scratch,
            compiler_params=pltpu.CompilerParams(vmem_limit_bytes=24 * 1024 * 1024),
            cost_estimate=pl.CostEstimate(
                flops=2 * 3 * halves * 128 * 128 * COLS,
                bytes_accessed=2**20 * halves,
                transcendentals=0,
            ),
        )(bins, *operands)

    def held(n):
        return pltpu.VMEM((n, ROWS, COLS), jnp.float32)

    def pick(*places):
        return [v[k] for k in places for v in (mine, last)]

    planes = call(first_kernel, 4, [], [spectra, left, *pick(0, 3, 4, 6)])
    totals = call(second_kernel, 3, [held(6)], [planes, left, coefs, *pick(2, 5, 7)])
    pieces = [
        held(2),
        pltpu.VMEM((TWIN, ROWS, COLS), jnp.bfloat16),
        pltpu.SemaphoreType.DMA((ROWS // GROUP,)),
    ]
    operands = [planes, left, coefs, *pick(1), totals]
    return call(
        third_kernel, 1, pieces, operands, pl.BlockSpec(memory_space=pl.ANY), jnp.bfloat16
    )


def tables(filters, offsets, strip, bins, yl):
    lag = np.arange(64, dtype=np.int64)[:, None] * (FIRST_BIN + np.arange(FREQ))[None, :] % NT
    lag_angle = lag * (2.0 * math.pi / NT)
    response_cos = jnp.dot(filters, jnp.asarray(np.cos(lag_angle), jnp.float32), precision=HI)
    response_sin = jnp.dot(filters, jnp.asarray(np.sin(lag_angle), jnp.float32), precision=HI)
    a_real, a_imag = strip[0], strip[1]
    rc, rs = response_cos.T[:, :, None], response_sin.T[:, :, None]
    real = a_real * rc + a_imag * rs
    imag = a_imag * rc - a_real * rs
    re_first = jnp.concatenate([real, -imag], axis=2)
    im_first = jnp.concatenate([imag, real], axis=2)
    re_last = jnp.concatenate([-imag, real], axis=2)
    im_last = jnp.concatenate([real, imag], axis=2)
    left = jnp.where(
        yl == 0,
        jnp.concatenate([re_first, im_first], axis=1),
        jnp.concatenate([re_last, im_last], axis=1),
    )
    times = offsets[:, None] + jnp.arange(TWIN, dtype=jnp.int32)[None, :]
    phase = times[:, :, None] * (FIRST_BIN + bins)[None, None, :] & (NT - 1)
    angle = phase.astype(jnp.float32) * (2.0 * math.pi / NT)
    coefs = jnp.stack([jnp.cos(angle), -jnp.sin(angle)], axis=3).reshape(ROWS, 64)
    return left, coefs


def scatter(rows):
    members = [(f - 2 * c) % 4 * 2 + c for c in range(2) for f in range(4)]
    return lax.all_to_all(rows, ("x", "yl"), 0, 0, axis_index_groups=[members], tiled=True)


def exchange(panels):
    def send(v, way):
        axis, pairs = {
            "on": ("x", [(i, (i + 1) % 4) for i in range(4)]),
            "back": ("x", [(i, (i - 1) % 4) for i in range(4)]),
            "y": ("yl", [(0, 1), (1, 0)]),
        }[way]
        return lax.ppermute(v, axis, pairs)

    near = [(send(own, "on"), send(own, "back"), send(own, "y")) for own in panels]
    mid = [(send(a, "on"), send(c, "back"), send(a, "y")) for a, _, c in near]
    far = [
        send(d, "y") if i == 0 else send(e, "back") for i, (d, e, _) in enumerate(mid)
    ]
    return [
        [own, g, d, c, a, e, b, f]
        for own, (a, b, c), (d, e, f), g in zip(panels, near, mid, far)
    ]


def shards(spectra, panels, filters, offsets):
    x, z, yl = lax.axis_index("x"), lax.axis_index("z"), lax.axis_index("yl")
    other_first = panels[1] == LAST
    other = jnp.where(other_first, panels[0], panels[1])
    ox, oz, oy = place_of(other)
    lx, lz, ly = place_of(LAST)
    strip = strips(spectra, other)
    strip = owned(strip, opposite(strip, "c"), other, "c")
    arrived = scatter(spectra.reshape(2 * FREQ, ROWS, COLS))
    arrived, strip = lax.optimization_barrier((arrived, strip))
    spot = (oy * 4 + ((ox + 2 * oy) & 3)).astype(jnp.uint32)
    mine = lax.dynamic_index_in_dim(arrived, spot, 0, keepdims=False)
    last = arrived[ly * 4 + (lx + 2 * ly) % 4]

    def branch(root):
        return lambda a, b, block: (leap(a, root), leap(b, lz), opposite(block, "yh"))

    leapt, last_leapt, across = lax.switch(
        oz, [branch(r) for r in range(8)], mine, last, strip
    )
    mine, last = land(mine, leapt, oz, z), land(last, last_leapt, lz, z)
    strip = owned(strip, across, other, "yh").reshape(2, FREQ, ROWS, 2 * ROWS)
    mine, last = steps(mine, oz, z, False), steps(last, lz, z, True)
    last, strip = lax.optimization_barrier((last, strip))
    mine, last = exchange([mine, last])
    bins = (x + 2 * yl + jnp.array([0, 2, 3, 1], jnp.int32)) & 3
    left, coefs = tables(filters, offsets, strip, bins, yl)
    return synthesise(bins, spectra, left, coefs, mine, last)


def solution(mesh):
    fine = Mesh(mesh.devices.reshape(4, 8, 2, 2, 2), ("x", "z", "yl", "yh", "c"))
    src, rcv = ("x", "z", "yl"), ("yh", "c")
    return jax.shard_map(
        shards,
        mesh=fine,
        in_specs=(P(None, None, src, rcv), P(), P(src, None), P(src)),
        out_specs=P(None, src, rcv),
        check_vma=False,
    )
```

```python
import math

import jax
import jax.numpy as jnp
import numpy as np
from jax import lax
from jax.experimental import pallas as pl
from jax.experimental.pallas import tpu as pltpu
from jax.sharding import Mesh
from jax.sharding import PartitionSpec as P

TWIN = 8
NT = 2048
FIRST_BIN = 64
FREQ = 4
ROWS = 64
COLS = 1024
GROUP = 16
LAST = 63
HI = lax.Precision.HIGHEST


def place_of(panel):
    return panel >> 4, (panel >> 1) & 7, panel & 1


def leap(v, root):
    up = lax.ppermute(v, "z", [(root, (root + 3) % 8)])
    down = lax.ppermute(v, "z", [(root, (root - 3) % 8)])
    return up, down


def land(v, leapt, root, z):
    d = (z - root) & 7
    return jnp.where(d == 0, v, jnp.where(d == 3, leapt[0], leapt[1]))


def steps(held, root, z, exact):
    def pairs(step, away):
        senders = [(root + k) % 8 for k in away] if exact else range(8)
        return [(k, (k + step) % 8) for k in senders]

    after = lax.ppermute(held, "z", pairs(1, (0, 3, 5)))
    before = lax.ppermute(held, "z", pairs(-1, (0, 3)))
    d = (z - root) & 7
    from_after = (d == 1) | (d == 4) | (d == 6)
    from_before = (d == 2) | (d == 7)
    return jnp.where(from_after, after, jnp.where(from_before, before, held))


def strips(spectra, panel):
    flat = spectra.reshape(2 * FREQ, ROWS, COLS)
    start = (panel.astype(jnp.uint32) & 15) * ROWS
    block = jnp.concatenate(
        [lax.dynamic_slice_in_dim(flat, start, ROWS, 2), flat[:, :, COLS - ROWS :]], axis=2
    )
    return block


def opposite(block, axis):
    return lax.ppermute(block, axis, [(0, 1), (1, 0)])


def owned(block, other, panel, axis):
    is_first = lax.broadcasted_iota(jnp.int32, (1, 1, 2 * ROWS), 2) < ROWS
    bit = panel >> 4 & 1 if axis == "c" else panel >> 5
    keep = jnp.where(is_first, bit, 1) == lax.axis_index(axis)
    return jnp.where(keep, block, other)


def partial(sets, bins, x_ref, l_ref, coef_ref, block_refs, before_ref, d_ref, store):
    for n, i in enumerate(sets):
        b = jnp.concatenate([r[...] for r in block_refs[4 * n : 4 * n + 4]], axis=0)
        high = b.astype(jnp.bfloat16)
        low = (b - high.astype(jnp.float32)).astype(jnp.bfloat16)
        f = bins[i]
        left = l_ref[f]
        left_high = left.astype(jnp.bfloat16)
        left_low = (left - left_high.astype(jnp.float32)).astype(jnp.bfloat16)
        both = jnp.dot(
            jnp.concatenate([left_high, left_low], axis=0),
            high,
            preferred_element_type=jnp.float32,
        )
        rest = jnp.dot(left_high, low, preferred_element_type=jnp.float32)
        product = both[: 2 * ROWS] + (both[2 * ROWS :] + rest)
        d_ref[2 * n] = x_ref[0, f] - product[:ROWS]
        d_ref[2 * n + 1] = x_ref[1, f] - product[ROWS:]
    for first in range(0, ROWS, GROUP):
        rows = slice(first, first + GROUP)
        spectrum = [d_ref[k, rows, :] for k in range(2 * len(sets))]
        for u in range(TWIN):
            total = None if before_ref is None else before_ref[u, rows, :]
            for k, value in enumerate(spectrum):
                at = u * 8 + 2 * sets[0] + k
                term = value * coef_ref[rows, at : at + 1]
                total = term if total is None else total + term
            store(u, rows, total)


def early_kernel(bins, x_ref, l_ref, coef_ref, *refs):
    block_refs, o_ref, d_ref = refs[:12], refs[12], refs[13]

    def store(u, rows, total):
        o_ref[u, rows, :] = total

    partial((1, 2, 3), bins, x_ref, l_ref, coef_ref, block_refs, None, d_ref, store)


def late_kernel(bins, x_ref, l_ref, coef_ref, *refs):
    block_refs, before_ref, o_ref, d_ref = refs[:4], refs[4], refs[5], refs[6]

    def store(u, rows, total):
        o_ref[u, rows, :] = total.astype(o_ref.dtype)

    partial((0,), bins, x_ref, l_ref, coef_ref, block_refs, before_ref, d_ref, store)


def synthesise(bins, spectra, left, coefs, blocks):
    vmem = pl.BlockSpec(memory_space=pltpu.VMEM)

    def call(body, sets, dtype, operands):
        return pl.pallas_call(
            body,
            in_specs=[pl.BlockSpec(memory_space=pltpu.SMEM), *[vmem] * len(operands)],
            out_specs=vmem,
            out_shape=jax.ShapeDtypeStruct((TWIN, ROWS, COLS), dtype),
            scratch_shapes=[pltpu.VMEM((2 * sets, ROWS, COLS), jnp.float32)],
            compiler_params=pltpu.CompilerParams(vmem_limit_bytes=24 * 1024 * 1024),
            cost_estimate=pl.CostEstimate(
                flops=2 * 3 * sets * 128 * 256 * COLS,
                bytes_accessed=2 * 2**20 * sets,
                transcendentals=0,
            ),
        )(bins, *operands)

    early = call(early_kernel, 3, jnp.float32, [spectra, left, coefs, *blocks[4:]])
    return call(
        late_kernel, 1, jnp.bfloat16, [spectra, left, coefs, *blocks[:4], early]
    )


def tables(filters, offsets, strip, bins, yl):
    lag = np.arange(64, dtype=np.int64)[:, None] * (FIRST_BIN + np.arange(FREQ))[None, :] % NT
    lag_angle = lag * (2.0 * math.pi / NT)
    response_cos = jnp.dot(filters, jnp.asarray(np.cos(lag_angle), jnp.float32), precision=HI)
    response_sin = jnp.dot(filters, jnp.asarray(np.sin(lag_angle), jnp.float32), precision=HI)
    a_real, a_imag = strip[0], strip[1]
    rc, rs = response_cos.T[:, :, None], response_sin.T[:, :, None]
    real = a_real * rc + a_imag * rs
    imag = a_imag * rc - a_real * rs
    re_first = jnp.concatenate([real, -imag], axis=2)
    im_first = jnp.concatenate([imag, real], axis=2)
    re_last = jnp.concatenate([-imag, real], axis=2)
    im_last = jnp.concatenate([real, imag], axis=2)
    left = jnp.where(
        yl == 0,
        jnp.concatenate([re_first, im_first], axis=1),
        jnp.concatenate([re_last, im_last], axis=1),
    )
    times = offsets[:, None] + jnp.arange(TWIN, dtype=jnp.int32)[None, :]
    phase = times[:, :, None] * (FIRST_BIN + bins)[None, None, :] & (NT - 1)
    angle = phase.astype(jnp.float32) * (2.0 * math.pi / NT)
    coefs = jnp.stack([jnp.cos(angle), -jnp.sin(angle)], axis=3).reshape(ROWS, 64)
    return left, coefs


def scatter(rows):
    members = [(f - 2 * c) % 4 * 2 + c for c in range(2) for f in range(4)]
    return lax.all_to_all(rows, ("x", "yl"), 0, 0, axis_index_groups=[members], tiled=True)


def exchange(panels):
    def send(v, way):
        axis, pairs = {
            "on": ("x", [(i, (i + 1) % 4) for i in range(4)]),
            "back": ("x", [(i, (i - 1) % 4) for i in range(4)]),
            "y": ("yl", [(0, 1), (1, 0)]),
        }[way]
        return lax.ppermute(v, axis, pairs)

    near = [(send(own, "on"), send(own, "back"), send(own, "y")) for own in panels]
    mid = [(send(a, "on"), send(c, "back"), send(a, "y")) for a, _, c in near]
    far = [
        send(d, "y") if i == 0 else send(e, "back") for i, (d, e, _) in enumerate(mid)
    ]
    return [
        [own, g, d, c, a, e, b, f]
        for own, (a, b, c), (d, e, f), g in zip(panels, near, mid, far)
    ]


def shards(spectra, panels, filters, offsets):
    x, z, yl = lax.axis_index("x"), lax.axis_index("z"), lax.axis_index("yl")
    other_first = panels[1] == LAST
    other = jnp.where(other_first, panels[0], panels[1])
    ox, oz, oy = place_of(other)
    lx, lz, ly = place_of(LAST)
    strip = strips(spectra, other)
    strip = owned(strip, opposite(strip, "c"), other, "c")
    arrived = scatter(spectra.reshape(2 * FREQ, ROWS, COLS))
    arrived, strip = lax.optimization_barrier((arrived, strip))
    spot = (oy * 4 + ((ox + 2 * oy) & 3)).astype(jnp.uint32)
    mine = lax.dynamic_index_in_dim(arrived, spot, 0, keepdims=False)
    last = arrived[ly * 4 + (lx + 2 * ly) % 4]

    def branch(root):
        return lambda a, b, block: (leap(a, root), leap(b, lz), opposite(block, "yh"))

    leapt, last_leapt, across = lax.switch(
        oz, [branch(r) for r in range(8)], mine, last, strip
    )
    mine, last = land(mine, leapt, oz, z), land(last, last_leapt, lz, z)
    strip = owned(strip, across, other, "yh").reshape(2, FREQ, ROWS, 2 * ROWS)
    mine, last = steps(mine, oz, z, False), steps(last, lz, z, True)
    last, strip = lax.optimization_barrier((last, strip))
    mine, last = exchange([mine, last])
    blocks = [v for pair in zip(mine, last) for v in pair]
    bins = (x + 2 * yl + jnp.array([0, 2, 3, 1], jnp.int32)) & 3
    left, coefs = tables(filters, offsets, strip, bins, yl)
    return synthesise(bins, spectra, left, coefs, blocks)


def solution(mesh):
    fine = Mesh(mesh.devices.reshape(4, 8, 2, 2, 2), ("x", "z", "yl", "yh", "c"))
    src, rcv = ("x", "z", "yl"), ("yh", "c")
    return jax.shard_map(
        shards,
        mesh=fine,
        in_specs=(P(None, None, src, rcv), P(), P(src, None), P(src)),
        out_specs=P(None, src, rcv),
        check_vma=False,
    )
```

```python
import math

import jax
import jax.numpy as jnp
import numpy as np
from jax import lax
from jax.experimental import pallas as pl
from jax.experimental.pallas import tpu as pltpu
from jax.sharding import Mesh
from jax.sharding import PartitionSpec as P

TWIN = 8
NT = 2048
FIRST_BIN = 64
FREQ = 4
ROWS = 64
COLS = 1024
GROUP = 16
LAST = 63
HI = lax.Precision.HIGHEST


def place_of(panel):
    return panel >> 4, (panel >> 1) & 7, panel & 1


def leap(v, root):
    up = lax.ppermute(v, "z", [(root, (root + 3) % 8)])
    down = lax.ppermute(v, "z", [(root, (root - 3) % 8)])
    return up, down


def land(v, leapt, root, z):
    d = (z - root) & 7
    return jnp.where(d == 0, v, jnp.where(d == 3, leapt[0], leapt[1]))


def steps(held, root, z, exact):
    def pairs(step, away):
        senders = [(root + k) % 8 for k in away] if exact else range(8)
        return [(k, (k + step) % 8) for k in senders]

    after = lax.ppermute(held, "z", pairs(1, (0, 3, 5)))
    before = lax.ppermute(held, "z", pairs(-1, (0, 3)))
    d = (z - root) & 7
    from_after = (d == 1) | (d == 4) | (d == 6)
    from_before = (d == 2) | (d == 7)
    return jnp.where(from_after, after, jnp.where(from_before, before, held))


def strips(spectra, panel):
    flat = spectra.reshape(2 * FREQ, ROWS, COLS)
    start = (panel.astype(jnp.uint32) & 15) * ROWS
    block = jnp.concatenate(
        [lax.dynamic_slice_in_dim(flat, start, ROWS, 2), flat[:, :, COLS - ROWS :]], axis=2
    )
    return block


def opposite(block, axis):
    return lax.ppermute(block, axis, [(0, 1), (1, 0)])


def owned(block, other, panel, axis):
    is_first = lax.broadcasted_iota(jnp.int32, (1, 1, 2 * ROWS), 2) < ROWS
    bit = panel >> 4 & 1 if axis == "c" else panel >> 5
    keep = jnp.where(is_first, bit, 1) == lax.axis_index(axis)
    return jnp.where(keep, block, other)


def partial(sets, bins, x_ref, l_ref, coef_ref, block_refs, before_ref, d_ref, store):
    for n, i in enumerate(sets):
        b = jnp.concatenate([r[...] for r in block_refs[4 * n : 4 * n + 4]], axis=0)
        high = b.astype(jnp.bfloat16)
        low = (b - high.astype(jnp.float32)).astype(jnp.bfloat16)
        f = bins[i]
        left = l_ref[f]
        left_high = left.astype(jnp.bfloat16)
        left_low = (left - left_high.astype(jnp.float32)).astype(jnp.bfloat16)
        both = jnp.dot(
            jnp.concatenate([left_high, left_low], axis=0),
            high,
            preferred_element_type=jnp.float32,
        )
        rest = jnp.dot(left_high, low, preferred_element_type=jnp.float32)
        product = both[: 2 * ROWS] + (both[2 * ROWS :] + rest)
        d_ref[2 * n] = x_ref[0, f] - product[:ROWS]
        d_ref[2 * n + 1] = x_ref[1, f] - product[ROWS:]
    for first in range(0, ROWS, GROUP):
        rows = slice(first, first + GROUP)
        spectrum = [d_ref[k, rows, :] for k in range(2 * len(sets))]
        for u in range(TWIN):
            total = None if before_ref is None else before_ref[u, rows, :]
            for k, value in enumerate(spectrum):
                at = u * 8 + 2 * sets[0] + k
                term = value * coef_ref[rows, at : at + 1]
                total = term if total is None else total + term
            store(u, rows, total)


def early_kernel(bins, x_ref, l_ref, coef_ref, *refs):
    block_refs, o_ref, d_ref = refs[:12], refs[12], refs[13]

    def store(u, rows, total):
        o_ref[u, rows, :] = total

    partial((1, 2, 3), bins, x_ref, l_ref, coef_ref, block_refs, None, d_ref, store)


def late_kernel(bins, x_ref, l_ref, coef_ref, *refs):
    block_refs, before_ref, o_ref, d_ref = refs[:4], refs[4], refs[5], refs[6]

    def store(u, rows, total):
        o_ref[u, rows, :] = total.astype(o_ref.dtype)

    partial((0,), bins, x_ref, l_ref, coef_ref, block_refs, before_ref, d_ref, store)


def synthesise(bins, spectra, left, coefs, blocks):
    vmem = pl.BlockSpec(memory_space=pltpu.VMEM)

    def call(body, sets, dtype, operands):
        return pl.pallas_call(
            body,
            in_specs=[pl.BlockSpec(memory_space=pltpu.SMEM), *[vmem] * len(operands)],
            out_specs=vmem,
            out_shape=jax.ShapeDtypeStruct((TWIN, ROWS, COLS), dtype),
            scratch_shapes=[pltpu.VMEM((2 * sets, ROWS, COLS), jnp.float32)],
            compiler_params=pltpu.CompilerParams(vmem_limit_bytes=24 * 1024 * 1024),
            cost_estimate=pl.CostEstimate(
                flops=2 * 3 * sets * 128 * 256 * COLS,
                bytes_accessed=2 * 2**20 * sets,
                transcendentals=0,
            ),
        )(bins, *operands)

    early = call(early_kernel, 3, jnp.float32, [spectra, left, coefs, *blocks[4:]])
    return call(
        late_kernel, 1, jnp.bfloat16, [spectra, left, coefs, *blocks[:4], early]
    )


def tables(filters, offsets, strip, bins, yl):
    lag = np.arange(64, dtype=np.int64)[:, None] * (FIRST_BIN + np.arange(FREQ))[None, :] % NT
    lag_angle = lag * (2.0 * math.pi / NT)
    response_cos = jnp.dot(filters, jnp.asarray(np.cos(lag_angle), jnp.float32), precision=HI)
    response_sin = jnp.dot(filters, jnp.asarray(np.sin(lag_angle), jnp.float32), precision=HI)
    a_real, a_imag = strip[0], strip[1]
    rc, rs = response_cos.T[:, :, None], response_sin.T[:, :, None]
    real = a_real * rc + a_imag * rs
    imag = a_imag * rc - a_real * rs
    re_first = jnp.concatenate([real, -imag], axis=2)
    im_first = jnp.concatenate([imag, real], axis=2)
    re_last = jnp.concatenate([-imag, real], axis=2)
    im_last = jnp.concatenate([real, imag], axis=2)
    left = jnp.where(
        yl == 0,
        jnp.concatenate([re_first, im_first], axis=1),
        jnp.concatenate([re_last, im_last], axis=1),
    )
    times = offsets[:, None] + jnp.arange(TWIN, dtype=jnp.int32)[None, :]
    phase = times[:, :, None] * (FIRST_BIN + bins)[None, None, :] & (NT - 1)
    angle = phase.astype(jnp.float32) * (2.0 * math.pi / NT)
    coefs = jnp.stack([jnp.cos(angle), -jnp.sin(angle)], axis=3).reshape(ROWS, 64)
    return left, coefs


def scatter(rows):
    members = [(f - 2 * c) % 4 * 2 + c for c in range(2) for f in range(4)]
    return lax.all_to_all(rows, ("x", "yl"), 0, 0, axis_index_groups=[members], tiled=True)


def exchange(panels):
    def send(v, way):
        axis, pairs = {
            "on": ("x", [(i, (i + 1) % 4) for i in range(4)]),
            "back": ("x", [(i, (i - 1) % 4) for i in range(4)]),
            "y": ("yl", [(0, 1), (1, 0)]),
        }[way]
        return lax.ppermute(v, axis, pairs)

    near = [(send(own, "on"), send(own, "back"), send(own, "y")) for own in panels]
    mid = [(send(a, "on"), send(c, "back"), send(a, "y")) for a, _, c in near]
    far = [
        send(d, "y") if i == 0 else send(e, "back") for i, (d, e, _) in enumerate(mid)
    ]
    return [
        [own, g, d, c, a, e, b, f]
        for own, (a, b, c), (d, e, f), g in zip(panels, near, mid, far)
    ]


def shards(spectra, panels, filters, offsets):
    x, z, yl = lax.axis_index("x"), lax.axis_index("z"), lax.axis_index("yl")
    other_first = panels[1] == LAST
    other = jnp.where(other_first, panels[0], panels[1])
    ox, oz, oy = place_of(other)
    lx, lz, ly = place_of(LAST)
    strip = strips(spectra, other)
    strip = owned(strip, opposite(strip, "c"), other, "c")
    arrived = scatter(spectra.reshape(2 * FREQ, ROWS, COLS))
    arrived, strip = lax.optimization_barrier((arrived, strip))
    spot = (oy * 4 + ((ox + 2 * oy) & 3)).astype(jnp.uint32)
    mine = lax.dynamic_index_in_dim(arrived, spot, 0, keepdims=False)
    last = arrived[ly * 4 + (lx + 2 * ly) % 4]

    def branch(root):
        return lambda a, b, block: (leap(a, root), leap(b, lz), opposite(block, "yh"))

    leapt, last_leapt, across = lax.switch(
        oz, [branch(r) for r in range(8)], mine, last, strip
    )
    mine, last = land(mine, leapt, oz, z), land(last, last_leapt, lz, z)
    strip = owned(strip, across, other, "yh").reshape(2, FREQ, ROWS, 2 * ROWS)
    last, mine = exchange([steps(last, lz, z, True), steps(mine, oz, z, False)])
    blocks = [v for pair in zip(mine, last) for v in pair]
    bins = (x + 2 * yl + jnp.array([0, 2, 3, 1], jnp.int32)) & 3
    left, coefs = tables(filters, offsets, strip, bins, yl)
    return synthesise(bins, spectra, left, coefs, blocks)


def solution(mesh):
    fine = Mesh(mesh.devices.reshape(4, 8, 2, 2, 2), ("x", "z", "yl", "yh", "c"))
    src, rcv = ("x", "z", "yl"), ("yh", "c")
    return jax.shard_map(
        shards,
        mesh=fine,
        in_specs=(P(None, None, src, rcv), P(), P(src, None), P(src)),
        out_specs=P(None, src, rcv),
        check_vma=False,
    )
```
